32 devices in a mesh: seq: 8 (over z, y), wsh: 4 (over x, core).
Axes of the slice: x: 2, y: 2, z: 4, core: 2. Of those that a mesh axis runs over, the one named last changes fastest.
Arguments:
- hidden: bfloat16 [4, 2048, 2048], P('wsh', 'seq'), may hold values from -6 to 6
- teacher: bfloat16 [4, 2048, 2048], P('wsh', 'seq'), may hold values from -15 to 15
- cotangent: bfloat16 [4, 2048, 2048], P('wsh', 'seq'), may hold values from -6 to 6
- lengths: int32 [4], P('wsh'), may hold values from 1024 to 2048, as said below
- norm_gain: bfloat16 [2048], P('wsh'), may hold values from 0.5 to 1.5
- in_weight: bfloat16 [2048, 8192], P('wsh'), may hold values from -0.125 to 0.125
- conv_weight: bfloat16 [4, 4096], P(None, 'wsh'), may hold values from -3 to 3
- conv_bias: bfloat16 [4096], P('wsh'), may hold values from -3 to 3
- x_weight: bfloat16 [160, 4096], P(None, 'wsh'), may hold values from -0.09375 to 0.09375
- dt_weight: bfloat16 [128, 4096], P(None, 'wsh'), may hold values from -0.5 to 0.5
- dt_bias: bfloat16 [4096], P('wsh'), may hold values from -12 to -1
- a_log: bfloat16 [16, 4096], P(None, 'wsh'), may hold values from -1.3828125 to 1.3828125
- skip_gain: bfloat16 [4096], P('wsh'), may hold values from 0.5 to 1.5
- out_weight: bfloat16 [4096, 2048], P('wsh'), may hold values from -0.25 to 0.25
Outputs:
- output: bfloat16 [4, 2048, 2048], P('wsh', 'seq')
- loss: float32 [], replicated
- hidden_grad: bfloat16 [4, 2048, 2048], P('wsh', 'seq')
- norm_gain_grad: float32 [2048], P('wsh')
- in_weight_grad: float32 [2048, 8192], P('wsh')
- conv_weight_grad: float32 [4, 4096], P(None, 'wsh')
- conv_bias_grad: float32 [4096], P('wsh')
- x_weight_grad: float32 [160, 4096], P(None, 'wsh')
- dt_weight_grad: float32 [128, 4096], P(None, 'wsh')
- dt_bias_grad: float32 [4096], P('wsh')
- a_log_grad: float32 [16, 4096], P(None, 'wsh')
- skip_gain_grad: float32 [4096], P('wsh')
- out_weight_grad: float32 [4096, 2048], P('wsh')
The draws below stay inside these ranges and needn't reach their ends.
Inputs may be any that keep to these rules, and one draw needn't show every extreme that they name: lengths[s] counts the valid tokens at the start of sequence s; in every draw one sequence has all 2048 tokens valid.
All inputs are finite; a program needn't handle non-finite values.
Results may differ from the reference program's by a relative error of at most 0.012.
Values may be sent and summed in bfloat16 or wider, within the bound.
No kernel may reach another device: no remote copies, remote signals or barrier semaphores. Data moves between devices by JAX's collectives and lax.ppermute only.
A program may use at most 384 MiB of HBM per device.

```python
import math
import jax
import jax.numpy as jnp
from jax import lax

D = 2048
INNER = 4096
STATE = 16
DT_RANK = 128
CONV = 4
SCAN_BLOCK = 32
PROJ = 160
LENGTH = 2048
SEQS = 4


def draw_teacher(key, part):
    place = jnp.arange(LENGTH, dtype=jnp.float32) / LENGTH
    base = jnp.clip(jax.random.normal(key, (SEQS, LENGTH, D), jnp.float32), -5.0, 5.0)
    ramp = 1.0 + 2.0 * place
    return (base * ramp[None, :, None]).astype(jnp.bfloat16)


def draw_lengths(key, part):
    key_len, key_full = jax.random.split(jax.random.fold_in(key, 11))
    drawn = jax.random.randint(key_len, (SEQS,), LENGTH // 2, LENGTH + 1)
    chosen = jax.random.randint(key_full, (), 0, SEQS)
    return jnp.where(jnp.arange(SEQS) == chosen, LENGTH, drawn).astype(jnp.int32)


def draw_dt_bias(key, part):
    key_pick, key_slow, key_fast = jax.random.split(jax.random.fold_in(key, 7), 3)
    share = 0.5
    slow = jax.random.uniform(key_pick, (INNER,), jnp.float32) < share
    slow_rate = jnp.exp(jax.random.uniform(key_slow, (INNER,), jnp.float32, 0.0, math.log(16.0))) / LENGTH
    fast_rate = jnp.exp(jax.random.uniform(key_fast, (INNER,), jnp.float32, math.log(0.005), math.log(0.02)))
    chosen_rate = jnp.where(slow, slow_rate, fast_rate)
    return jnp.log(jnp.expm1(chosen_rate)).astype(jnp.bfloat16)


def block_scale(rng, dims, cuts, least, largest):
    level, own = 1.0, jax.random.fold_in(rng, 6)
    for position, shards_of in cuts:
        heights = jnp.exp(jax.random.uniform(jax.random.fold_in(own, position), (shards_of,), jnp.float32, least / len(cuts), largest / len(cuts)))
        level = level * jnp.repeat(heights, dims[position] // shards_of).reshape([-1 if axis == position else 1 for axis in range(len(dims))])
    return level


def centred(key, dims, scale, bound, cuts=(), kind=jnp.bfloat16):
    array = jax.random.normal(key, dims, jnp.float32) * scale
    if len(cuts) > 0:
        array = block_scale(key, dims, cuts, -0.22, 0.18) * array
    return jnp.clip(array, min=-bound, max=bound).astype(kind)


def setup_inputs(seed: int = 0) -> dict:
    seeds = jax.random.split(jax.random.key(seed), 15)
    return {
        "hidden": centred(seeds[0], (SEQS, LENGTH, D), 1.0, 6.0, ((0, 4), (1, 8))),
        "teacher": draw_teacher(jax.random.fold_in(seeds[14], 71), 0),
        "cotangent": centred(seeds[2], (SEQS, LENGTH, D), 1.0, 6.0, ((0, 4), (1, 8))),
        "lengths": draw_lengths(jax.random.fold_in(seeds[14], 71), 0),
        "norm_gain": jnp.clip(1.0 + 0.1 * jax.random.normal(seeds[4], (D,), jnp.float32), 0.5, 1.5).astype(jnp.bfloat16),
        "in_weight": centred(seeds[5], (D, 2 * INNER), D ** -0.5, 0.125, ((0, 4),)),
        "conv_weight": centred(seeds[6], (CONV, INNER), CONV ** -0.5, 3.0, ((1, 4),)),
        "conv_bias": centred(seeds[7], (INNER,), 0.5, 3.0, ((0, 4),)),
        "x_weight": centred(seeds[8], (PROJ, INNER), INNER ** -0.5, 0.09375, ((1, 4),)),
        "dt_weight": centred(seeds[9], (DT_RANK, INNER), DT_RANK ** -0.5, 0.5, ((1, 4),)),
        "dt_bias": draw_dt_bias(jax.random.fold_in(seeds[14], 71), 0),
        "a_log": jnp.clip(jax.random.uniform(seeds[11], (STATE, INNER), jnp.float32, -1.3828125, 1.3828125) * block_scale(seeds[11], (STATE, INNER), ((1, 4),), -0.4, 0.0), -1.3828125, 1.3828125).astype(jnp.bfloat16),
        "skip_gain": jnp.clip(0.5 + 1.0 * jax.random.uniform(seeds[12], (INNER,), jnp.float32) ** block_scale(seeds[12], (INNER,), ((0, 4),), -0.2, 0.2), 0.5, 1.5).astype(jnp.bfloat16),
        "out_weight": centred(seeds[13], (INNER, D), (INNER // 8) ** -0.5, 0.25, ((0, 4),)),
    }


NORM_EPS = 1e-05
FULL_PRECISION = lax.Precision.HIGHEST

@jax.custom_vjp
def low(v):
    return lax.optimization_barrier(v.astype(jnp.bfloat16)).astype(jnp.float32)

@jax.custom_vjp
def low_back(v):
    return v

def low_keep(v):
    return (low(v), None)

def low_pass(kept, grad):
    return (grad,)

def back_keep(v):
    return (v, None)

def back_low(kept, grad):
    return (low(grad),)
low.defvjp(low_keep, low_pass)
low_back.defvjp(back_keep, back_low)

def silu_value(v):
    return v * jax.nn.sigmoid(v)

def block_combine(first, second):
    return (first[0] * second[0], second[0] * first[1] + second[1])

def sequence_scan(step, activated, b_in, c_out, rate):
    count_blocks = step.shape[0] // SCAN_BLOCK

    def to_blocks(v):
        return v.reshape((count_blocks, SCAN_BLOCK) + v.shape[1:])

    @jax.checkpoint
    def one_block(carry, pieces):
        step_k, act_k, b_k, c_k = pieces
        decay = jnp.exp(step_k[:, None, :] * rate[None])
        drive = (step_k * act_k)[:, None, :] * b_k[:, :, None]
        decay_cum, drive_cum = lax.associative_scan(block_combine, (decay, drive), axis=0)
        states = decay_cum * carry[None] + drive_cum
        return (states[-1], lax.optimization_barrier(jnp.sum(states * c_k[:, :, None], axis=1)))
    begin = jnp.zeros(rate.shape, jnp.float32)
    _, outs = lax.scan(one_block, begin, (to_blocks(step), to_blocks(activated), to_blocks(b_in), to_blocks(c_out)))
    return outs.reshape(step.shape)

def forward(rows_in, gain, input_projection, conv_taps, conv_shift, x_proj, dt_proj, bias_dt, log_rate, skip, output_projection, mask):
    inner = output_projection.shape[0]
    scale = lax.rsqrt(lax.optimization_barrier(jnp.mean(rows_in * rows_in, axis=-1, keepdims=True)) + NORM_EPS)
    normalized_input = low(rows_in * scale * gain)
    joint_projection = low_back(jnp.einsum('zuw,wx->zux', normalized_input, input_projection, precision=FULL_PRECISION))
    x_in = low(joint_projection[:, :, :inner] * mask[:, :, None])
    z_part = joint_projection[:, :, inner:]
    padded = jnp.pad(x_in, ((0, 0), (CONV - 1, 0), (0, 0)))
    conv_out = conv_shift + jnp.zeros_like(x_in)
    for tap in range(CONV):
        conv_out = conv_out + conv_taps[tap] * padded[:, tap:tap + LENGTH]
    activated = low(silu_value(conv_out))
    proj = low(low_back(jnp.einsum('sle,pe->slp', activated, x_proj, precision=FULL_PRECISION)))
    dt_low = proj[:, :, :DT_RANK]
    b_in = proj[:, :, DT_RANK:DT_RANK + STATE]
    c_out = proj[:, :, DT_RANK + STATE:]
    pre = low_back(jnp.einsum('slr,re->sle', dt_low, dt_proj, precision=FULL_PRECISION))
    step = jax.nn.softplus(pre + bias_dt)
    rate = -jnp.exp(log_rate)
    scanned = lax.map(lambda item: sequence_scan(item[0], item[1], item[2], item[3], rate), (step, activated, b_in, c_out))
    mixed = scanned + skip * activated
    gated_output = low(mixed * silu_value(z_part))
    residual_branch = low_back(jnp.einsum('oxw,wq->oxq', gated_output, output_projection, precision=FULL_PRECISION))
    return rows_in + residual_branch

def reference(hidden, teacher, cotangent, lengths, norm_gain, in_weight, conv_weight, conv_bias, x_weight, dt_weight, dt_bias, a_log, skip_gain, out_weight):
    positions = jnp.arange(LENGTH, dtype=jnp.int32)
    mask = (positions[None, :] < lengths[:, None]).astype(jnp.float32)
    count = jnp.sum(mask)
    target = teacher.astype(jnp.float32)

    def objective(rows_in, gain, input_projection, conv_taps, conv_shift, x_proj, dt_proj, bias_dt, log_rate, skip, output_projection):
        full = forward(rows_in, gain, input_projection, conv_taps, conv_shift, x_proj, dt_proj, bias_dt, log_rate, skip, output_projection, mask)
        miss = full - target
        loss = jnp.sum(mask[:, :, None] * miss * miss) / (D * count)
        return (full, loss)
    primals = (hidden.astype(jnp.float32), norm_gain.astype(jnp.float32), in_weight.astype(jnp.float32), conv_weight.astype(jnp.float32), conv_bias.astype(jnp.float32), x_weight.astype(jnp.float32), dt_weight.astype(jnp.float32), dt_bias.astype(jnp.float32), a_log.astype(jnp.float32), skip_gain.astype(jnp.float32), out_weight.astype(jnp.float32))
    (full, loss), pullback = jax.vjp(objective, *primals)
    grads = pullback((cotangent.astype(jnp.float32), jnp.ones((), jnp.float32)))
    return (full.astype(jnp.bfloat16), loss, grads[0].astype(jnp.bfloat16), grads[1], grads[2], grads[3], grads[4], grads[5], grads[6], grads[7], grads[8], grads[9], grads[10])
```

```python
from functools import partial

import jax
import jax.numpy as jnp
from jax import lax
from jax.experimental import pallas as pl
from jax.experimental.pallas import tpu as pltpu
from jax.sharding import PartitionSpec as P

F32 = jnp.float32
BF16 = jnp.bfloat16
NORM_EPS = 1e-05
LOG2E = 1.4426950408889634
LN2 = 0.6931471805599453
GROUP = 8
CHUNK = 32
HALO = 16
VMEM_LIMIT = 56 * 1024 * 1024
ROWS_FIRST = (((0,), (0,)), ((), ()))
COLS_LAST = (((1,), (1,)), ((), ()))
PLAIN = (((1,), (0,)), ((), ()))


def product(left, right, dims):
    return lax.dot_general(left, right, dims, preferred_element_type=F32)


def silu_value(v):
    return v * jax.nn.sigmoid(v)


def silu_slope(v):
    sigma = jax.nn.sigmoid(v)
    return sigma * (1.0 + v * (1.0 - sigma))


def kernel_params():
    return pltpu.CompilerParams(vmem_limit_bytes=VMEM_LIMIT)


def widen(bc_ref, row, size, rep_ref):
    for t0 in range(0, bc_ref.shape[1], 128):
        x=bc_ref[row:row+size, t0:t0+128]
        for k in range(128):
            rep_ref[t0+k]=jnp.broadcast_to(x[:, k:k+1], (size, 128))

def tiled(x, width):
    return jnp.concatenate([x]*(width//128), axis=1)

def put_fold(fold_ref,k,v):
    for i in range(v.shape[1]//128):
        fold_ref[i,8*k:8*k+8,:]=v[:,128*i:128*i+128]

def get_fold(fold_ref):
    def tree(x):
        while len(x)>1: x=[a+b for a,b in zip(x[::2],x[1::2])]
        return x[0]
    return jnp.concatenate([tree([fold_ref[i,pl.ds(r,GROUP,stride=8),:] for r in range(8)]) for i in range(fold_ref.shape[0])],axis=1)

def p1_kernel(step_ref, act_ref, bc_ref, rate_ref, last_ref, total_ref, dx_ref, brep_ref, *, eb, n):
    widen(bc_ref,0,n,brep_ref)
    step=step_ref[...]
    dx_ref[...]=step*act_ref[...].astype(F32)
    total_ref[0]=jnp.sum(step,axis=0,keepdims=True)
    tokens,width=step_ref.shape
    for e in range(0,width,eb):
        sl=slice(e,e+eb)
        rate=rate_ref[:,sl]
        def group(g,h):
            base=pl.multiple_of(g*GROUP,GROUP)
            s8=step_ref[pl.ds(base,GROUP),sl]
            x8=dx_ref[pl.ds(base,GROUP),sl]
            for k in range(GROUP):
                d=jnp.exp2(rate*s8[k:k+1])
                h=d*h+tiled(brep_ref[base+k],eb)*x8[k:k+1]
            return h
        last_ref[0,:,sl]=lax.fori_loop(0,tokens//GROUP,group,jnp.zeros((n,eb),F32))

def p1(step,act,bc,rate,seqs,eb=512):
    rows,width=step.shape; tokens=rows//seqs; n=rate.shape[0]
    return pl.pallas_call(partial(p1_kernel,eb=eb,n=n),grid=(seqs,),
        in_specs=[pl.BlockSpec((tokens,width),lambda s:(s,0)),pl.BlockSpec((tokens,width),lambda s:(s,0)),
                  pl.BlockSpec((bc.shape[0],tokens),lambda s:(0,s)),pl.BlockSpec((n,width),lambda s:(0,0))],
        out_specs=[pl.BlockSpec((1,n,width),lambda s:(s,0,0)),pl.BlockSpec((1,1,width),lambda s:(s,0,0))],
        out_shape=[jax.ShapeDtypeStruct((seqs,n,width),F32),jax.ShapeDtypeStruct((seqs,1,width),F32)],
        scratch_shapes=[pltpu.VMEM((tokens,width),F32),pltpu.VMEM((tokens,n,128),F32)],
        compiler_params=kernel_params())(step,act,bc,rate)

def p2_kernel(step_ref, act_ref, z_ref, bc_ref, rate_ref, skip_ref, carry_ref, mixed_ref, gated_ref, starts_ref, dx_ref, fold_ref, brep_ref, crep_ref, *, eb, n):
    widen(bc_ref,0,n,brep_ref)
    widen(bc_ref,n,n,crep_ref)
    dx_ref[...]=step_ref[...]*act_ref[...].astype(F32)
    tokens,width=step_ref.shape
    for e in range(0,width,eb):
        sl=slice(e,e+eb)
        rate=rate_ref[:,sl]
        def chunk(c,h):
            starts_ref[0,c,:,sl]=h
            def group(j,h):
                g=c*(CHUNK//GROUP)+j
                base=pl.multiple_of(g*GROUP,GROUP)
                s8=step_ref[pl.ds(base,GROUP),sl]
                x8=dx_ref[pl.ds(base,GROUP),sl]
                for k in range(GROUP):
                    d=jnp.exp2(rate*s8[k:k+1])
                    h=d*h+tiled(brep_ref[base+k],eb)*x8[k:k+1]
                    p=tiled(crep_ref[base+k],eb)*h
                    put_fold(fold_ref,k,sum(p[8*i:8*i+8] for i in range(n//8)))
                mixed_ref[pl.ds(base,GROUP),sl]=get_fold(fold_ref)
                return h
            return lax.fori_loop(0,CHUNK//GROUP,group,h)
        lax.fori_loop(0,tokens//CHUNK,chunk,carry_ref[0,:,sl])
    def gate(i,_):
        rows=pl.ds(pl.multiple_of(i*16,16),16)
        m=mixed_ref[rows,:]+skip_ref[...]*act_ref[rows,:].astype(F32)
        mixed_ref[rows,:]=m
        z=z_ref[rows,:]
        gated_ref[rows,:]=(m*(z*jax.nn.sigmoid(z))).astype(BF16)
        return 0
    lax.fori_loop(0,tokens//16,gate,0)

def p2(step,act,z,bc,rate,skip,carry,seqs,eb=512):
    rows,width=step.shape; tokens=rows//seqs; n=rate.shape[0]
    blk=pl.BlockSpec((tokens,width),lambda s:(s,0))
    nch=tokens//CHUNK
    return pl.pallas_call(partial(p2_kernel,eb=eb,n=n),grid=(seqs,),
        in_specs=[blk,blk,blk,pl.BlockSpec((bc.shape[0],tokens),lambda s:(0,s)),pl.BlockSpec((n,width),lambda s:(0,0)),
                  pl.BlockSpec((1,width),lambda s:(0,0)),pl.BlockSpec((1,n,width),lambda s:(s,0,0))],
        out_specs=[blk,blk,pl.BlockSpec((1,nch,n,width),lambda s:(s,0,0,0))],
        out_shape=[jax.ShapeDtypeStruct((rows,width),F32),jax.ShapeDtypeStruct((rows,width),BF16),jax.ShapeDtypeStruct((seqs,nch,n,width),F32)],
        scratch_shapes=[pltpu.VMEM((tokens,width),F32),pltpu.VMEM((eb//128,64,128),F32),pltpu.VMEM((tokens,n,128),F32),pltpu.VMEM((tokens,n,128),F32)],
        compiler_params=kernel_params())(step,act,z,bc,rate,skip,carry)

def b1_kernel(step_ref, dy_ref, bc_ref, rate_ref, first_ref, crep_ref, *, eb, n):
    widen(bc_ref,n,n,crep_ref)
    tokens,width=step_ref.shape
    for e in range(0,width,eb):
        sl=slice(e,e+eb)
        rate=rate_ref[:,sl]
        def group(j,h):
            g=tokens//GROUP-1-j
            base=pl.multiple_of(g*GROUP,GROUP)
            s8=step_ref[pl.ds(base,GROUP),sl]
            y8=dy_ref[pl.ds(base,GROUP),sl]
            for k in reversed(range(GROUP)):
                h=jnp.exp2(rate*s8[k:k+1])*(h+tiled(crep_ref[base+k],eb)*y8[k:k+1])
            return h
        first_ref[0,:,sl]=lax.fori_loop(0,tokens//GROUP,group,jnp.zeros((n,eb),F32))

def b1(step,dy,bc,rate,seqs,eb=512):
    rows,width=step.shape; tokens=rows//seqs; n=rate.shape[0]
    blk=pl.BlockSpec((tokens,width),lambda s:(s,0))
    return pl.pallas_call(partial(b1_kernel,eb=eb,n=n),grid=(seqs,),
        in_specs=[blk,blk,pl.BlockSpec((bc.shape[0],tokens),lambda s:(0,s)),pl.BlockSpec((n,width),lambda s:(0,0))],
        out_specs=pl.BlockSpec((1,n,width),lambda s:(s,0,0)),
        out_shape=jax.ShapeDtypeStruct((seqs,n,width),F32),
        scratch_shapes=[pltpu.VMEM((tokens,n,128),F32)],
        compiler_params=kernel_params())(step,dy,bc,rate)

def one_less_exp(s):
    return jnp.where(s<0.01, s*(1.0-s*(0.5-s*(1.0/6.0))), 1.0-jnp.exp(-s))

def b2_kernel(step_ref, act_ref, dy_ref, bc_ref, rate_ref, skip_ref, starts_ref, carry_ref,
              gpre_ref, gact_ref, gb_ref, gc_ref, alog_ref, dtb_ref,
              dx_ref, prev_ref, dec_ref, folda_ref, folds_ref, pb_ref, pc_ref, g_ref, brep_ref, crep_ref, *, eb, n):
    widen(bc_ref,0,n,brep_ref)
    widen(bc_ref,n,n,crep_ref)
    tokens,width=step_ref.shape
    nch=tokens//CHUNK; per=CHUNK//GROUP
    dx_ref[...]=step_ref[...]*act_ref[...].astype(F32)
    g_ref[...]=carry_ref[0]
    @pl.when(pl.program_id(0)==0)
    def _():
        alog_ref[...]=jnp.zeros_like(alog_ref)
        dtb_ref[...]=jnp.zeros_like(dtb_ref)
    ones=jnp.ones((8,128),F32)
    def chunk(cc,_):
        c=nch-1-cc
        for e in range(0,width,eb):
            sl=slice(e,e+eb)
            rate=rate_ref[:,sl]
            def redo(j,h):
                g=c*per+j
                base=pl.multiple_of(g*GROUP,GROUP)
                s8=step_ref[pl.ds(base,GROUP),sl]
                x8=dx_ref[pl.ds(base,GROUP),sl]
                for k in range(GROUP):
                    d=jnp.exp2(rate*s8[k:k+1])
                    prev_ref[j*GROUP+k]=h
                    dec_ref[j*GROUP+k]=d
                    h=d*h+tiled(brep_ref[base+k],eb)*x8[k:k+1]
                return h
            last=lax.fori_loop(0,per,redo,starts_ref[0,c,:,sl])
            def back(jj,carry):
                h,alog,after=carry
                j=per-1-jj
                g=c*per+j
                base=pl.multiple_of(g*GROUP,GROUP)
                s8=step_ref[pl.ds(base,GROUP),sl]
                x8=dx_ref[pl.ds(base,GROUP),sl]
                y8=dy_ref[pl.ds(base,GROUP),sl]
                for k in reversed(range(GROUP)):
                    s=s8[k:k+1]
                    g_state=tiled(crep_ref[base+k],eb)*y8[k:k+1]+h
                    prev=prev_ref[j*GROUP+k]
                    pc=after*y8[k:k+1]
                    pb=g_state*x8[k:k+1]
                    al=g_state*tiled(brep_ref[base+k],eb)
                    h=g_state*dec_ref[j*GROUP+k]
                    q=h*prev
                    alog=alog+q*s
                    qs=q*rate
                    pcs=sum(pc[:,i:i+128] for i in range(0,eb,128))
                    pbs=sum(pb[:,i:i+128] for i in range(0,eb,128))
                    rows=pl.ds(pl.multiple_of((j*GROUP+k)*n,n),n)
                    if e==0:
                        pc_ref[rows,:]=pcs; pb_ref[rows,:]=pbs
                    else:
                        pc_ref[rows,:]+=pcs; pb_ref[rows,:]+=pbs
                    put_fold(folda_ref,k,sum(al[8*i:8*i+8] for i in range(n//8)))
                    put_fold(folds_ref,k,sum(qs[8*i:8*i+8] for i in range(n//8)))
                    after=prev
                gact_ref[pl.ds(base,GROUP),sl]=get_fold(folda_ref)
                dx_ref[pl.ds(base,GROUP),sl]=get_fold(folds_ref)
                return h,alog,after
            h,alog,_u=lax.fori_loop(0,per,back,(g_ref[:,sl],jnp.zeros((n,eb),F32),last))
            g_ref[:,sl]=h
            alog_ref[:,sl]+=alog
        for j in range(per):
            part=pb_ref[j*128:(j+1)*128,:]
            gb_ref[0,pl.ds(c*per+j,1),:]=lax.dot_general(ones,part,(((1,),(1,)),((),())),precision=lax.Precision.HIGHEST,preferred_element_type=F32)[0:1]
            part=pc_ref[j*128:(j+1)*128,:]
            gc_ref[0,pl.ds(c*per+j,1),:]=lax.dot_general(ones,part,(((1,),(1,)),((),())),precision=lax.Precision.HIGHEST,preferred_element_type=F32)[0:1]
        return 0
    lax.fori_loop(0,nch,chunk,0)
    def finish(i,acc):
        rows=pl.ds(pl.multiple_of(i*16,16),16)
        s=step_ref[rows,:]; along=gact_ref[rows,:]
        a=act_ref[rows,:].astype(F32)
        garg=(dx_ref[rows,:]*LN2+a*along)*one_less_exp(s)
        gpre_ref[rows,:]=garg.astype(BF16)
        gact_ref[rows,:]=dy_ref[rows,:]*skip_ref[...]+s*along
        return acc+jnp.sum(garg.reshape(2,8,width),axis=0)
    acc=lax.fori_loop(0,tokens//16,finish,jnp.zeros((8,width),F32))
    dtb_ref[...]+=acc

def b2(step,act,dy,bc,rate,skip,starts,carry,seqs,eb=512):
    rows,width=step.shape; tokens=rows//seqs; n=rate.shape[0]
    blk=pl.BlockSpec((tokens,width),lambda s:(s,0))
    nch=tokens//CHUNK
    full=lambda shape: pl.BlockSpec(shape,lambda s:(0,)*len(shape))
    red=pl.BlockSpec((1,tokens//GROUP,128),lambda s:(s,0,0))
    return pl.pallas_call(partial(b2_kernel,eb=eb,n=n),grid=(seqs,),
        in_specs=[blk,blk,blk,pl.BlockSpec((bc.shape[0],tokens),lambda s:(0,s)),full((n,width)),full((1,width)),
                  pl.BlockSpec((1,nch,n,width),lambda s:(s,0,0,0)),pl.BlockSpec((1,n,width),lambda s:(s,0,0))],
        out_specs=[blk,blk,red,red,full((n,width)),full((8,width))],
        out_shape=[jax.ShapeDtypeStruct((rows,width),BF16),jax.ShapeDtypeStruct((rows,width),F32),
                   jax.ShapeDtypeStruct((seqs,tokens//GROUP,128),F32),jax.ShapeDtypeStruct((seqs,tokens//GROUP,128),F32),
                   jax.ShapeDtypeStruct((n,width),F32),jax.ShapeDtypeStruct((8,width),F32)],
        scratch_shapes=[pltpu.VMEM((tokens,width),F32),pltpu.VMEM((CHUNK,n,eb),F32),pltpu.VMEM((CHUNK,n,eb),F32),
                        pltpu.VMEM((eb//128,64,128),F32),pltpu.VMEM((eb//128,64,128),F32),pltpu.VMEM((CHUNK*n,128),F32),pltpu.VMEM((CHUNK*n,128),F32),
                        pltpu.VMEM((n,width),F32),pltpu.VMEM((tokens,n,128),F32),pltpu.VMEM((tokens,n,128),F32)],
        compiler_params=kernel_params())(step,act,dy,bc,rate,skip,starts,carry)


def swap(v, bit):
    return jax.tree.map(
        lambda a: lax.ppermute(a, "wsh", [(i, i ^ bit) for i in range(lax.axis_size("wsh"))]), v
    )


def shifted(v, distance):
    count = lax.axis_size("seq")
    route = [(i - distance, i) for i in range(count) if 0 <= i - distance < count]
    return jax.tree.map(lambda a: lax.ppermute(a, "seq", route), v)


def spread_out(v):
    one = swap(v, 1)
    two = swap(v, 2)
    return [v, one, two, swap(two, 1)]


def sum_to_owner(parts, own_cast=BF16):
    got1, got3 = swap((parts[1].astype(own_cast), parts[3].astype(own_cast)), 1)
    mine = parts[0] + got1.astype(F32)
    other = (parts[2] + got3.astype(F32)).astype(own_cast)
    return mine + swap(other, 2).astype(F32)


def crossed(v, bit):
    got = jnp.split(swap(v, bit), lax.axis_size("wsh"), axis=1)
    return jnp.concatenate([got[r ^ bit] for r in range(len(got))], axis=1)


def sum_all(v):
    v = v + crossed(v, 1)
    return v + crossed(v.astype(BF16), 2).astype(F32)


def carried(total, state, rate, reverse):
    count = lax.axis_size("seq")
    sign = -1 if reverse else 1
    total, state = shifted((total, state), sign)
    hop = 1
    while hop < count:
        got_total, got_state = shifted((total, state), sign * hop)
        state = state + jnp.exp2(rate[None] * total) * got_state
        total = total + got_total
        hop *= 2
    return state


def reduced(rows):
    return lax.psum_scatter(rows, "seq", scatter_dimension=0, tiled=True)


def local(
    hidden,
    teacher,
    cotangent,
    lengths,
    norm_gain,
    in_weight,
    conv_weight,
    conv_bias,
    x_weight,
    dt_weight,
    dt_bias,
    a_log,
    skip_gain,
    out_weight,
):
    me = lax.axis_index("wsh")
    place = lax.axis_index("seq")
    seqs = lax.axis_size("wsh")
    seq_count = lax.axis_size("seq")
    tokens, width = hidden.shape[1:]
    inner = out_weight.shape[0]
    depth = in_weight.shape[0]
    states = a_log.shape[0]
    rank = dt_weight.shape[0]
    taps = conv_weight.shape[0]
    rows = seqs * tokens

    def slots(pieces):
        return [lax.dynamic_index_in_dim(pieces, me ^ r, 0, False) for r in range(seqs)]

    all_lengths = lax.all_gather(lengths, "wsh", axis=0, tiled=True)
    gain = lax.all_gather(norm_gain, "wsh", axis=0, tiled=True).astype(F32)
    whole = place * 0 + seq_count * tokens
    count = jnp.sum(jnp.minimum(all_lengths, whole)).astype(F32)
    slot_lengths = jnp.stack(slots(all_lengths))
    positions = place * tokens + lax.iota(jnp.int32, tokens)
    valid = (positions[None, :] < slot_lengths[:, None]).astype(F32)
    halo_positions = place * tokens - HALO + lax.iota(jnp.int32, HALO + tokens)
    halo_valid = (halo_positions[None, :] < slot_lengths[:, None]).astype(F32)

    rows_in = hidden[0].astype(F32)
    scale = lax.rsqrt(jnp.mean(rows_in * rows_in, axis=1, keepdims=True) + NORM_EPS)
    normed_own = (rows_in * scale * gain).astype(BF16)
    before = shifted(normed_own[tokens - HALO :], 1)
    normed = jnp.stack(spread_out(jnp.concatenate([before, normed_own], axis=0)))
    normed_tokens = normed[:, HALO:].reshape(rows, width)

    split = in_weight.reshape(depth, 2, seqs, inner)
    mine = [lax.dynamic_index_in_dim(split, me ^ r, 2, False) for r in range(seqs)]
    got = [mine[0]] + [swap(mine[r], r) for r in range(1, seqs)]
    columns = jnp.stack([lax.dynamic_index_in_dim(jnp.stack(got), me ^ j, 0, False) for j in range(seqs)])
    x_columns = columns[:, :, 0].reshape(width, inner)
    z_columns = columns[:, :, 1].reshape(width, inner)

    x_both = product(normed.reshape(seqs * (HALO + tokens), width), x_columns, PLAIN)
    x_in = (x_both.reshape(seqs, HALO + tokens, inner) * halo_valid[:, :, None]).astype(BF16)
    padded = x_in[:, HALO - (taps - 1) :].astype(F32)
    conv_f = conv_weight.astype(F32)
    conv_out = conv_bias.astype(F32) + sum(
        conv_f[tap] * padded[:, tap : tap + tokens] for tap in range(taps)
    )
    conv_out = conv_out.reshape(rows, inner)
    act = silu_value(conv_out).astype(BF16)
    act_f = act.astype(F32)
    proj = sum_all(product(x_weight, act, COLS_LAST)).astype(BF16)
    dt_low = proj[:rank]
    bc = proj[rank:].astype(F32)
    step = jax.nn.softplus(product(dt_low, dt_weight, ROWS_FIRST) + dt_bias.astype(F32))
    log_rate = a_log.astype(F32)
    rate = -jnp.exp(log_rate) * LOG2E
    skip = skip_gain.astype(F32)[None]

    last, total = p1(step, act, bc, rate, seqs)
    z_part = product(normed_tokens, z_columns, PLAIN)
    carry = carried(total, last, rate, False)
    mixed, gated, starts = p2(step, act, z_part, bc, rate, skip, carry, seqs)
    out_parts = product(gated, out_weight, PLAIN).reshape(seqs, tokens, width)
    full = rows_in + sum_to_owner(out_parts)
    own_valid = valid[0][:, None]
    miss = full - teacher[0].astype(F32)
    loss = lax.psum(jnp.sum(own_valid * miss * miss), ("seq", "wsh")) / (width * count)
    g_full = cotangent[0].astype(F32) + 2.0 / (width * count) * own_valid * miss
    g_branch = jnp.stack(spread_out(g_full.astype(BF16))).reshape(rows, width)

    g_gated = product(g_branch, out_weight, COLS_LAST)
    g_mixed = g_gated * silu_value(z_part)
    g_z = (g_gated * mixed * silu_slope(z_part)).astype(BF16)
    out_grad = product(gated, g_branch, ROWS_FIRST)
    out_owned = lax.all_gather(reduced(out_grad.astype(BF16)), "seq", axis=0, tiled=True)
    skip_grad = jnp.sum(g_mixed * act_f, axis=0)

    first = b1(step, g_mixed, bc, rate, seqs)
    carry_back = carried(total, first, rate, True)
    g_pre, g_act_part, g_b, g_c, rate_sum, dt_bias_sum = b2(
        step, act, g_mixed, bc, rate, skip, starts, carry_back, seqs
    )
    g_dt_low = product(dt_weight, g_pre, COLS_LAST)
    g_proj = sum_all(
        jnp.concatenate([g_dt_low, g_b.reshape(rows, states).T, g_c.reshape(rows, states).T], axis=0)
    ).astype(BF16)
    g_act = g_act_part + product(g_proj, x_weight, ROWS_FIRST)
    g_conv = (g_act * silu_slope(conv_out)).reshape(seqs, tokens, inner)
    after = shifted(g_conv[:, : taps - 1].astype(BF16), -1).astype(F32)
    g_padded = jnp.concatenate([g_conv, after], axis=1)
    g_x_in = sum(conv_f[tap] * g_padded[:, taps - 1 - tap : taps - 1 - tap + tokens] for tap in range(taps))
    g_x = (g_x_in * valid[:, :, None]).astype(BF16).reshape(rows, inner)
    conv_grad = [jnp.sum(g_conv * padded[:, tap : tap + tokens], axis=(0, 1)) for tap in range(taps)]
    small = jnp.concatenate(
        [
            product(g_proj, act, PLAIN),
            product(dt_low, g_pre, PLAIN),
            rate_sum * (rate * LN2),
            jnp.stack(conv_grad + [jnp.sum(g_conv, axis=(0, 1)), jnp.sum(dt_bias_sum, axis=0), skip_grad]),
        ],
        axis=0,
    )
    small = lax.psum(small, "seq")
    cut = [0]
    for piece in (x_weight.shape[0], rank, states, taps, 1, 1, 1):
        cut.append(cut[-1] + piece)
    x_grad, dt_grad, log_rate_grad, conv_grad, conv_bias_grad, dt_bias_grad, skip_grad = [
        small[a:b] for a, b in zip(cut, cut[1:])
    ]

    def in_rows(grad):
        piece = depth // seq_count
        grad = grad.astype(BF16).reshape(seqs, seq_count, piece, inner)
        share = reduced(jnp.swapaxes(grad, 0, 1).reshape(width, inner))
        share = slots(share.reshape(seqs, piece, inner))
        got = jnp.stack([share[0]] + [swap(share[r], r) for r in range(1, seqs)])
        row = jnp.concatenate(slots(got), axis=1)
        return lax.all_gather(row, "seq", axis=0, tiled=True).astype(F32)

    in_z = in_rows(product(normed_tokens, g_z, ROWS_FIRST))
    in_x = in_rows(product(normed_tokens, g_x, ROWS_FIRST))
    in_grad = jnp.concatenate([in_x, in_z], axis=1)
    g_normed_parts = product(g_z, z_columns, COLS_LAST) + product(g_x, x_columns, COLS_LAST)
    g_normed = sum_to_owner(g_normed_parts.reshape(seqs, tokens, width))
    gain_grad = lax.psum(jnp.sum(g_normed * rows_in * scale, axis=0), ("seq", "wsh"))
    gain_grad = lax.dynamic_slice_in_dim(gain_grad, me * norm_gain.shape[0], norm_gain.shape[0])
    weighted = g_normed * gain
    g_rows = (
        g_full
        + scale * weighted
        - rows_in * scale * scale * scale * jnp.mean(weighted * rows_in, axis=1, keepdims=True)
    )
    return (
        full[None].astype(BF16),
        loss,
        g_rows[None].astype(BF16),
        gain_grad,
        in_grad,
        conv_grad,
        conv_bias_grad[0],
        x_grad,
        dt_grad,
        dt_bias_grad[0],
        log_rate_grad,
        skip_grad[0],
        out_owned.astype(F32),
    )


def solution(mesh):
    rows = P("wsh", "seq", None)
    first, second = P("wsh", None), P(None, "wsh")
    one = P("wsh")
    return jax.shard_map(
        local,
        mesh=mesh,
        in_specs=(
            rows, rows, rows, one, one, first, second, one, second, second, one, second, one, first,
        ),
        out_specs=(
            rows, P(), rows, one, first, second, one, second, second, one, second, one, first,
        ),
        check_vma=False,
    )
```

```python
from functools import partial

import jax
import jax.numpy as jnp
from jax import lax
from jax.experimental import pallas as pl
from jax.experimental.pallas import tpu as pltpu
from jax.sharding import PartitionSpec as P

F32 = jnp.float32
BF16 = jnp.bfloat16
NORM_EPS = 1e-05
LOG2E = 1.4426950408889634
LN2 = 0.6931471805599453
GROUP = 8
CHUNK = 32
HALO = 16
VMEM_LIMIT = 56 * 1024 * 1024
ROWS_FIRST = (((0,), (0,)), ((), ()))
COLS_LAST = (((1,), (1,)), ((), ()))
PLAIN = (((1,), (0,)), ((), ()))


def product(left, right, dims):
    return lax.dot_general(left, right, dims, preferred_element_type=F32)


def silu_value(v):
    return v * jax.nn.sigmoid(v)


def silu_slope(v):
    sigma = jax.nn.sigmoid(v)
    return sigma * (1.0 + v * (1.0 - sigma))


def kernel_params():
    return pltpu.CompilerParams(vmem_limit_bytes=VMEM_LIMIT)


def cost(microseconds):
    return pl.CostEstimate(flops=int(microseconds * 1e9), bytes_accessed=0, transcendentals=0)


def widen(bc_ref, row, size, rep_ref):
    ones = jnp.ones((128, 128), BF16)
    lane = lax.broadcasted_iota(jnp.int32, (size, 128), 1)
    part = 32

    def block(i, _):
        t0 = pl.multiple_of(i * 128, 128)
        x = bc_ref[row : row + size, pl.ds(t0, 128)]
        for j in range(0, 128, part):
            picked = jnp.concatenate([jnp.where(lane == k, x, 0.0) for k in range(j, j + part)], axis=0)
            wide = jnp.dot(picked.astype(BF16), ones, preferred_element_type=F32)
            rep_ref[pl.ds(t0 + j, part)] = wide.reshape(part, size, 128)
        return 0

    lax.fori_loop(0, bc_ref.shape[1] // 128, block, 0)


def tiled(x, width):
    return jnp.concatenate([x]*(width//128), axis=1)

def put_fold(fold_ref,k,v):
    for i in range(v.shape[1]//128):
        fold_ref[i,8*k:8*k+8,:]=v[:,128*i:128*i+128]

def get_fold(fold_ref):
    def tree(x):
        while len(x)>1: x=[a+b for a,b in zip(x[::2],x[1::2])]
        return x[0]
    return jnp.concatenate([tree([fold_ref[i,pl.ds(r,GROUP,stride=8),:] for r in range(8)]) for i in range(fold_ref.shape[0])],axis=1)

def p1_kernel(step_ref, act_ref, bc_ref, rate_ref, last_ref, total_ref, dx_ref, brep_ref, *, eb, n):
    widen(bc_ref,0,n,brep_ref)
    step=step_ref[...]
    dx_ref[...]=step*act_ref[...].astype(F32)
    total_ref[0]=jnp.sum(step,axis=0,keepdims=True)
    tokens,width=step_ref.shape
    for e in range(0,width,eb):
        sl=slice(e,e+eb)
        rate=rate_ref[:,sl]
        def group(g,h):
            base=pl.multiple_of(g*GROUP,GROUP)
            s8=step_ref[pl.ds(base,GROUP),sl]
            x8=dx_ref[pl.ds(base,GROUP),sl]
            for k in range(GROUP):
                d=jnp.exp2(rate*s8[k:k+1])
                h=d*h+tiled(brep_ref[base+k],eb)*x8[k:k+1]
            return h
        last_ref[0,:,sl]=lax.fori_loop(0,tokens//GROUP,group,jnp.zeros((n,eb),F32))

def p1(first, step, act, bc, rate, tokens, eb=512):
    width = step.shape[1]
    n = rate.shape[0]
    blk = pl.BlockSpec((tokens, width), lambda s: (first + s, 0))
    return pl.pallas_call(
        partial(p1_kernel, eb=eb, n=n),
        grid=(2,),
        in_specs=[
            blk,
            blk,
            pl.BlockSpec((bc.shape[0], tokens), lambda s: (0, first + s)),
            pl.BlockSpec((n, width), lambda s: (0, 0)),
        ],
        out_specs=[
            pl.BlockSpec((1, n, width), lambda s: (s, 0, 0)),
            pl.BlockSpec((1, 1, width), lambda s: (s, 0, 0)),
        ],
        out_shape=[jax.ShapeDtypeStruct((2, n, width), F32), jax.ShapeDtypeStruct((2, 1, width), F32)],
        scratch_shapes=[pltpu.VMEM((tokens, width), F32), pltpu.VMEM((tokens, n, 128), F32)],
        cost_estimate=cost(9),
        compiler_params=kernel_params(),
    )(step, act, bc, rate)


def p2_kernel(step_ref, act_ref, z_ref, bc_ref, rate_ref, skip_ref, carry_ref, mixed_ref, gated_ref, starts_ref, dx_ref, fold_ref, brep_ref, crep_ref, *, eb, n):
    widen(bc_ref,0,n,brep_ref)
    widen(bc_ref,n,n,crep_ref)
    dx_ref[...]=step_ref[...]*act_ref[...].astype(F32)
    tokens,width=step_ref.shape
    for e in range(0,width,eb):
        sl=slice(e,e+eb)
        rate=rate_ref[:,sl]
        def chunk(c,h):
            starts_ref[0,c,:,sl]=h
            def group(j,h):
                g=c*(CHUNK//GROUP)+j
                base=pl.multiple_of(g*GROUP,GROUP)
                s8=step_ref[pl.ds(base,GROUP),sl]
                x8=dx_ref[pl.ds(base,GROUP),sl]
                for k in range(GROUP):
                    d=jnp.exp2(rate*s8[k:k+1])
                    h=d*h+tiled(brep_ref[base+k],eb)*x8[k:k+1]
                    p=tiled(crep_ref[base+k],eb)*h
                    put_fold(fold_ref,k,sum(p[8*i:8*i+8] for i in range(n//8)))
                mixed_ref[pl.ds(base,GROUP),sl]=get_fold(fold_ref)
                return h
            return lax.fori_loop(0,CHUNK//GROUP,group,h)
        lax.fori_loop(0,tokens//CHUNK,chunk,carry_ref[0,:,sl])
    def gate(i,_):
        rows=pl.ds(pl.multiple_of(i*16,16),16)
        m=mixed_ref[rows,:]+skip_ref[...]*act_ref[rows,:].astype(F32)
        mixed_ref[rows,:]=m
        z=z_ref[rows,:]
        gated_ref[rows,:]=(m*(z*jax.nn.sigmoid(z))).astype(BF16)
        return 0
    lax.fori_loop(0,tokens//16,gate,0)

def p2(first, step, act, z, bc, rate, skip, carry, tokens, eb=512):
    width = step.shape[1]
    n = rate.shape[0]
    nch = tokens // CHUNK
    blk = pl.BlockSpec((tokens, width), lambda s: (first + s, 0))
    out = pl.BlockSpec((tokens, width), lambda s: (s, 0))
    rep = pltpu.VMEM((tokens, n, 128), F32)
    return pl.pallas_call(
        partial(p2_kernel, eb=eb, n=n),
        grid=(2,),
        in_specs=[
            blk,
            blk,
            blk,
            pl.BlockSpec((bc.shape[0], tokens), lambda s: (0, first + s)),
            pl.BlockSpec((n, width), lambda s: (0, 0)),
            pl.BlockSpec((1, width), lambda s: (0, 0)),
            pl.BlockSpec((1, n, width), lambda s: (s, 0, 0)),
        ],
        out_specs=[out, out, pl.BlockSpec((1, nch, n, width), lambda s: (s, 0, 0, 0))],
        out_shape=[
            jax.ShapeDtypeStruct((2 * tokens, width), F32),
            jax.ShapeDtypeStruct((2 * tokens, width), BF16),
            jax.ShapeDtypeStruct((2, nch, n, width), F32),
        ],
        scratch_shapes=[pltpu.VMEM((tokens, width), F32), pltpu.VMEM((eb // 128, 64, 128), F32), rep, rep],
        cost_estimate=cost(16),
        compiler_params=kernel_params(),
    )(step, act, z, bc, rate, skip, carry)


def b1_kernel(step_ref, dy_ref, bc_ref, rate_ref, first_ref, crep_ref, *, eb, n):
    widen(bc_ref,n,n,crep_ref)
    tokens,width=step_ref.shape
    for e in range(0,width,eb):
        sl=slice(e,e+eb)
        rate=rate_ref[:,sl]
        def group(j,h):
            g=tokens//GROUP-1-j
            base=pl.multiple_of(g*GROUP,GROUP)
            s8=step_ref[pl.ds(base,GROUP),sl]
            y8=dy_ref[pl.ds(base,GROUP),sl]
            for k in reversed(range(GROUP)):
                h=jnp.exp2(rate*s8[k:k+1])*(h+tiled(crep_ref[base+k],eb)*y8[k:k+1])
            return h
        first_ref[0,:,sl]=lax.fori_loop(0,tokens//GROUP,group,jnp.zeros((n,eb),F32))

def b1(first, step, dy, bc, rate, tokens, eb=512):
    width = step.shape[1]
    n = rate.shape[0]
    return pl.pallas_call(
        partial(b1_kernel, eb=eb, n=n),
        grid=(2,),
        in_specs=[
            pl.BlockSpec((tokens, width), lambda s: (first + s, 0)),
            pl.BlockSpec((tokens, width), lambda s: (s, 0)),
            pl.BlockSpec((bc.shape[0], tokens), lambda s: (0, first + s)),
            pl.BlockSpec((n, width), lambda s: (0, 0)),
        ],
        out_specs=pl.BlockSpec((1, n, width), lambda s: (s, 0, 0)),
        out_shape=jax.ShapeDtypeStruct((2, n, width), F32),
        scratch_shapes=[pltpu.VMEM((tokens, n, 128), F32)],
        cost_estimate=cost(9),
        compiler_params=kernel_params(),
    )(step, dy, bc, rate)


def one_less_exp(s):
    return jnp.where(s<0.01, s*(1.0-s*(0.5-s*(1.0/6.0))), 1.0-jnp.exp(-s))

def b2_kernel(step_ref, act_ref, dy_ref, bc_ref, rate_ref, skip_ref, starts_ref, carry_ref, *refs, eb, n):
    (gpre_ref, gact_ref, gb_ref, gc_ref, alog_ref, dtb_ref, dx_ref, prev_ref, dec_ref, folda_ref, folds_ref,
     pb_ref, pc_ref, g_ref, brep_ref, crep_ref) = refs[-16:]
    widen(bc_ref,0,n,brep_ref)
    widen(bc_ref,n,n,crep_ref)
    tokens,width=step_ref.shape
    nch=tokens//CHUNK; per=CHUNK//GROUP
    dx_ref[...]=step_ref[...]*act_ref[...].astype(F32)
    g_ref[...]=carry_ref[0]
    alog_ref[...]=jnp.zeros_like(alog_ref)
    ones=jnp.ones((8,128),F32)
    def chunk(cc,_):
        c=nch-1-cc
        for e in range(0,width,eb):
            sl=slice(e,e+eb)
            rate=rate_ref[:,sl]
            def redo(j,h):
                g=c*per+j
                base=pl.multiple_of(g*GROUP,GROUP)
                s8=step_ref[pl.ds(base,GROUP),sl]
                x8=dx_ref[pl.ds(base,GROUP),sl]
                for k in range(GROUP):
                    d=jnp.exp2(rate*s8[k:k+1])
                    prev_ref[j*GROUP+k]=h
                    dec_ref[j*GROUP+k]=d
                    h=d*h+tiled(brep_ref[base+k],eb)*x8[k:k+1]
                return h
            last=lax.fori_loop(0,per,redo,starts_ref[0,c,:,sl])
            def back(jj,carry):
                h,alog,after=carry
                j=per-1-jj
                g=c*per+j
                base=pl.multiple_of(g*GROUP,GROUP)
                s8=step_ref[pl.ds(base,GROUP),sl]
                x8=dx_ref[pl.ds(base,GROUP),sl]
                y8=dy_ref[pl.ds(base,GROUP),sl]
                for k in reversed(range(GROUP)):
                    s=s8[k:k+1]
                    g_state=tiled(crep_ref[base+k],eb)*y8[k:k+1]+h
                    prev=prev_ref[j*GROUP+k]
                    pc=after*y8[k:k+1]
                    pb=g_state*x8[k:k+1]
                    al=g_state*tiled(brep_ref[base+k],eb)
                    h=g_state*dec_ref[j*GROUP+k]
                    q=h*prev
                    alog=alog+q*s
                    qs=q*rate
                    pcs=sum(pc[:,i:i+128] for i in range(0,eb,128))
                    pbs=sum(pb[:,i:i+128] for i in range(0,eb,128))
                    rows=pl.ds(pl.multiple_of((j*GROUP+k)*n,n),n)
                    if e==0:
                        pc_ref[rows,:]=pcs; pb_ref[rows,:]=pbs
                    else:
                        pc_ref[rows,:]+=pcs; pb_ref[rows,:]+=pbs
                    put_fold(folda_ref,k,sum(al[8*i:8*i+8] for i in range(n//8)))
                    put_fold(folds_ref,k,sum(qs[8*i:8*i+8] for i in range(n//8)))
                    after=prev
                gact_ref[pl.ds(base,GROUP),sl]=get_fold(folda_ref)
                dx_ref[pl.ds(base,GROUP),sl]=get_fold(folds_ref)
                return h,alog,after
            h,alog,_u=lax.fori_loop(0,per,back,(g_ref[:,sl],jnp.zeros((n,eb),F32),last))
            g_ref[:,sl]=h
            alog_ref[0,:,sl]+=alog
        for j in range(per):
            part=pb_ref[j*128:(j+1)*128,:]
            gb_ref[0,pl.ds(c*per+j,1),:]=lax.dot_general(ones,part,(((1,),(1,)),((),())),precision=lax.Precision.HIGHEST,preferred_element_type=F32)[0:1]
            part=pc_ref[j*128:(j+1)*128,:]
            gc_ref[0,pl.ds(c*per+j,1),:]=lax.dot_general(ones,part,(((1,),(1,)),((),())),precision=lax.Precision.HIGHEST,preferred_element_type=F32)[0:1]
        return 0
    lax.fori_loop(0,nch,chunk,0)
    def finish(i,acc):
        rows=pl.ds(pl.multiple_of(i*16,16),16)
        s=step_ref[rows,:]; along=gact_ref[rows,:]
        a=act_ref[rows,:].astype(F32)
        garg=(dx_ref[rows,:]*LN2+a*along)*one_less_exp(s)
        gpre_ref[rows,:]=garg.astype(BF16)
        dy=dy_ref[rows,:]
        gact_ref[rows,:]=dy*skip_ref[...]+s*along
        return acc[0]+jnp.sum(garg.reshape(2,8,width),axis=0), acc[1]+jnp.sum((dy*a).reshape(2,8,width),axis=0)
    zero=jnp.zeros((8,width),F32)
    acc=lax.fori_loop(0,tokens//16,finish,(zero,zero))
    dtb_ref[0,0]=acc[0]
    dtb_ref[0,1]=acc[1]

def b2(first, count, filled, step, act, dy, bc, rate, skip, starts, carry, tokens, eb=512):
    base = first % 2
    rows, width = step.shape
    n = rate.shape[0]
    nch = tokens // CHUNK
    blk = pl.BlockSpec((tokens, width), lambda i: (first + i, 0))
    full = lambda shape: pl.BlockSpec(shape, lambda i: (0,) * len(shape))
    own = lambda shape: pl.BlockSpec((1, *shape[1:]), lambda i: (i,) + (0,) * (len(shape) - 1))
    red = (count, tokens // GROUP, 128)
    rep = pltpu.VMEM((tokens, n, 128), F32)
    held = pltpu.VMEM((CHUNK, n, eb), F32)
    fold = pltpu.VMEM((eb // 128, 64, 128), F32)
    part = pltpu.VMEM((CHUNK * n, 128), F32)
    extra = () if filled is None else tuple(filled)
    return pl.pallas_call(
        partial(b2_kernel, eb=eb, n=n),
        grid=(count,),
        in_specs=[
            blk,
            blk,
            pl.BlockSpec((tokens, width), lambda i: (base + i, 0)),
            pl.BlockSpec((bc.shape[0], tokens), lambda i: (0, first + i)),
            full((n, width)),
            full((1, width)),
            pl.BlockSpec((1, nch, n, width), lambda i: (base + i, 0, 0, 0)),
            pl.BlockSpec((1, n, width), lambda i: (base + i, 0, 0)),
        ]
        + [pl.BlockSpec(memory_space=pl.ANY)] * len(extra),
        out_specs=[blk, blk, own(red), own(red), own((count, n, width)), own((count, 2, 8, width))],
        out_shape=[
            jax.ShapeDtypeStruct((rows, width), BF16),
            jax.ShapeDtypeStruct((rows, width), F32),
            jax.ShapeDtypeStruct(red, F32),
            jax.ShapeDtypeStruct(red, F32),
            jax.ShapeDtypeStruct((count, n, width), F32),
            jax.ShapeDtypeStruct((count, 2, 8, width), F32),
        ],
        scratch_shapes=[
            pltpu.VMEM((tokens, width), F32),
            held,
            held,
            fold,
            fold,
            part,
            part,
            pltpu.VMEM((n, width), F32),
            rep,
            rep,
        ],
        input_output_aliases={8: 0, 9: 1} if extra else {},
        cost_estimate=cost(25 * count),
        compiler_params=kernel_params(),
    )(step, act, dy, bc, rate, skip, starts, carry, *extra)


def settle_kernel(at_ref, *refs, steps, base, blocks, cols, extra):
    out_ref = refs[-2] if extra else refs[-1]
    rows = out_ref.shape[0]
    i = base + pl.program_id(0)
    for d in range(2):
        for k in range(steps):
            ref = refs[d * steps + k]
            wide = ref.shape[1]

            @pl.when(at_ref[1 + d * steps + i] == k)
            def _():
                for r in range(blocks):
                    start = d * wide
                    if blocks > 1:
                        start = pl.multiple_of((at_ref[0] ^ r) * cols + start, 128)
                    out_ref[:, pl.ds(start, wide)] = ref[r * rows : (r + 1) * rows, :].astype(F32)
                if extra:
                    refs[-1][:, d * wide : (d + 1) * wide] = ref[blocks * rows :, :].astype(F32)


def settle(at, both, shape, blocks, cols, half=0, filled=None, extra=0, part=None):
    steps = len(both[0])
    rows, wide = both[0][0].shape
    piece = (rows - extra // steps) // blocks
    span = blocks * cols if blocks > 1 else 2 * wide
    given = [] if filled is None else [filled]
    count, base = (steps, 0) if part is None else (steps // 2, part * steps // 2)
    out_specs = [pl.BlockSpec((piece, span), lambda i, at_ref: (base + i, half))]
    out_shape = [jax.ShapeDtypeStruct(shape, F32)]
    if extra:
        out_specs.append(pl.BlockSpec((extra // steps, 2 * wide), lambda i, at_ref: (base + i, 0)))
        out_shape.append(jax.ShapeDtypeStruct((extra, 2 * wide), F32))
    whole = pl.BlockSpec((rows, wide), lambda i, at_ref: (0, 0))
    return pl.pallas_call(
        partial(settle_kernel, steps=steps, base=base, blocks=blocks, cols=cols, extra=extra),
        grid_spec=pltpu.PrefetchScalarGridSpec(
            num_scalar_prefetch=1,
            grid=(count,),
            in_specs=[whole] * (2 * steps) + [pl.BlockSpec(memory_space=pl.ANY)] * len(given),
            out_specs=out_specs,
        ),
        out_shape=out_shape,
        input_output_aliases={1 + 2 * steps: 0} if given else {},
        cost_estimate=cost(7 if part is None else 4),
        compiler_params=kernel_params(),
    )(at, *both[0], *both[1], *given)


def cut_rows_kernel(v_ref, *out_refs, cut):
    for ref, first in zip(out_refs, cut):
        ref[...] = v_ref[first : first + ref.shape[0], :]


def cut_rows(v, cut):
    whole = pl.BlockSpec(memory_space=pltpu.VMEM)
    sizes = [b - a for a, b in zip(cut, cut[1:])]
    return pl.pallas_call(
        partial(cut_rows_kernel, cut=cut),
        in_specs=[whole],
        out_specs=[whole] * len(sizes),
        out_shape=[jax.ShapeDtypeStruct((size, v.shape[1]), F32) for size in sizes],
        cost_estimate=cost(2),
        compiler_params=kernel_params(),
    )(v)


def spread_rows_kernel(*refs, count):
    out_ref = refs[-1]
    wide = refs[0].shape[1]
    for h in range(count):
        out_ref[:, h * wide : (h + 1) * wide] = refs[h][...].astype(F32)


def spread_rows(parts, shape, half=0, filled=None, part=None):
    rows, wide = parts[0].shape
    given = [] if filled is None else [filled]
    count, base = (8, 0) if part is None else (4, 4 * part)
    return pl.pallas_call(
        partial(spread_rows_kernel, count=len(parts)),
        grid=(count,),
        in_specs=[pl.BlockSpec((rows // 8, wide), lambda i: (base + i, 0))] * len(parts)
        + [pl.BlockSpec(memory_space=pl.ANY)] * len(given),
        out_specs=pl.BlockSpec((rows // 8, wide * len(parts)), lambda i: (base + i, half)),
        out_shape=jax.ShapeDtypeStruct(shape, F32),
        input_output_aliases={len(parts): 0} if given else {},
        cost_estimate=cost(4),
        compiler_params=kernel_params(),
    )(*parts, *given)


def join_kernel(at_ref, *refs):
    part, me = at_ref[0] % 4, at_ref[1]
    near_ref, next_ref, *far_refs, out_ref = refs
    depth = near_ref.shape[0]
    quarter = depth // 4
    half = quarter // 2

    def put(row, ref):
        out_ref[pl.ds(pl.multiple_of(row, half), ref.shape[0]), :] = ref[...]

    put(me * depth, near_ref)
    put((me ^ 1) * depth, next_ref)
    for k in range(2):
        start = (me ^ (2 + k)) * depth
        own, one, two, end, tail = far_refs[k::2]
        put(start + part * quarter, own)
        put(start + (part ^ 1) * quarter, one)
        put(start + (part ^ 2) * quarter, two)
        put(start + (part ^ 3) * quarter, end)
        put(start + (part ^ 3) * quarter + half, tail)


def join(at, pieces, rows):
    wide = pieces[0].shape[1]
    return pl.pallas_call(
        join_kernel,
        in_specs=[pl.BlockSpec(memory_space=pltpu.SMEM)] + [pl.BlockSpec(memory_space=pltpu.VMEM)] * len(pieces),
        out_specs=pl.BlockSpec(memory_space=pltpu.VMEM),
        out_shape=jax.ShapeDtypeStruct((rows, wide), BF16),
        cost_estimate=cost(4),
        compiler_params=kernel_params(),
    )(at, *pieces)


def swap(v, bit):
    return jax.tree.map(
        lambda a: lax.ppermute(a, "wsh", [(i, i ^ bit) for i in range(lax.axis_size("wsh"))]), v
    )


def shifted(v, distance):
    count = lax.axis_size("seq")
    route = [(i - distance, i) for i in range(count) if 0 <= i - distance < count]
    return jax.tree.map(lambda a: lax.ppermute(a, "seq", route), v)


def spread_out(v):
    one = swap(v, 1)
    two = swap(v, 2)
    return [v, one, two, swap(two, 1)]


def sum_to_owner(parts, own_cast=BF16):
    got1, got3 = swap((parts[1].astype(own_cast), parts[3].astype(own_cast)), 1)
    mine = parts[0] + got1.astype(F32)
    other = (parts[2] + got3.astype(F32)).astype(own_cast)
    return mine + swap(other, 2).astype(F32)


def crossed(v, bit):
    got = jnp.split(swap(v, bit), lax.axis_size("wsh"), axis=1)
    return jnp.concatenate([got[r ^ bit] for r in range(len(got))], axis=1)


def sum_all(v):
    v = v + crossed(v, 1)
    return v + crossed(v.astype(BF16), 2).astype(F32)


def hi_lo(v):
    hi = v.astype(BF16)
    return [hi, (v - hi.astype(F32)).astype(BF16)]


def carried_far(total, state, rate, reverse):
    count = lax.axis_size("seq")
    sign = -1 if reverse else 1
    total, state = shifted((total, state), sign)
    hop = 1
    while hop < count:
        got_total, got_state = shifted((total, state), sign * hop)
        state = state + jnp.exp2(rate[None] * total) * got_state
        total = total + got_total
        hop *= 2
    return state


class Carry:
    def __init__(self, total, state, rate, reverse):
        self.total, self.rate, self.reverse = total, rate, reverse
        self.near = lax.axis_size("seq") == 8
        if self.near:
            self.state = state
            self.moved = [seq_xor(self.packed(total, state), 1)]
        else:
            self.moved = [carried_far(total, state, rate, reverse)]

    def held(self, *others):
        count = len(self.moved)
        got = lax.optimization_barrier((*self.moved, *others))
        self.moved = list(got[:count])
        return got[count] if len(others) == 1 else got[count:]

    def packed(self, t, s):
        return jnp.concatenate([s.astype(BF16)] + hi_lo(t), axis=1)

    def opened(self, v):
        v = v.astype(F32)
        n = self.rate.shape[0]
        return v[:, n : n + 1] + v[:, n + 1 : n + 2], v[:, :n]

    def fall(self, t):
        return jnp.exp2(self.rate[None] * t)

    def second(self):
        if not self.near:
            return self
        place = lax.axis_index("seq")
        self.other_total, self.other_state = self.opened(self.moved[0])
        self.late = (place % 2 == 1) != self.reverse
        early_state = jnp.where(self.late, self.other_state, self.state)
        late_state = jnp.where(self.late, self.state, self.other_state)
        late_total = jnp.where(self.late, self.total, self.other_total)
        message = self.packed(self.total + self.other_total, self.fall(late_total) * early_state + late_state)
        sign = -1 if self.reverse else 1
        self.moved = [shifted(message, sign * 2 * k) for k in range(1, 4)]
        return self

    def result(self):
        if not self.near:
            return self.moved[0]
        got = [self.opened(v) for v in self.moved]
        carry = got[-1][1]
        for t, s in reversed(got[:-1]):
            carry = s + self.fall(t) * carry
        return jnp.where(self.late, self.fall(self.other_total) * carry + self.other_state, carry)


def seq_xor(v, bits):
    return lax.ppermute(v, "seq", [(i, i ^ bits) for i in range(lax.axis_size("seq"))])


def tied(v, *before):
    return lax.optimization_barrier((v, before))[0]


def at_index(v, index, axis):
    return lax.dynamic_index_in_dim(v, index, axis, False)


RING = (0, 2, 4, 6, 7, 5, 3, 1)


def ring_place():
    q = lax.axis_index("seq")
    return jnp.where(q % 2 == 0, q // 2, len(RING) - 1 - q // 2)


def ring_device(place):
    place = place % len(RING)
    return jnp.where(place < len(RING) // 2, 2 * place, 2 * len(RING) - 1 - 2 * place)


def ring_order():
    places = [RING.index(q) for q in range(len(RING))]
    p = ring_place()
    return [(p - k) % len(RING) for k in places] + [(k - p) % len(RING) for k in places]


class Ring:
    def __init__(self, share, between, own=None):
        self.share, self.between = share, between
        self.count, self.steps = len(RING), 0
        self.place = ring_place()
        if own is None:
            self.send([self.chunk(d, 1) for d in range(2)])
        else:
            self.steps = self.count - 1
            self.rounds = [[v] for v in own]
            self.send(own)

    def chunk(self, d, k):
        return self.share(d, ring_device(self.place + (k if d else self.count - k)))

    def send(self, held):
        self.steps += 1
        self.moving = []
        for d in range(2):
            route = [(RING[k], RING[(k + (-1 if d else 1)) % self.count]) for k in range(self.count)]
            self.moving.append(lax.ppermute(held[d], "seq", route))

    def step(self):
        k = self.steps + 1
        if k < self.count:
            self.send([self.added(d, k) for d in range(2)])
        elif k == self.count:
            own = self.between([self.added(d, k) for d in range(2)])
            self.rounds = [[v] for v in own]
            self.send(own)
        else:
            for d in range(2):
                self.rounds[d].append(self.moving[d])
            if k < 2 * self.count - 1:
                self.send(self.moving)

    def added(self, d, k):
        return (self.moving[d].astype(F32) + self.chunk(d, k).astype(F32)).astype(BF16)

    def result(self):
        return self.rounds

    def done(self):
        return self.steps >= self.count and len(self.rounds[0]) == self.count


def advance(rings, *others):
    count = 2 * len(rings)
    got = lax.optimization_barrier((*[v for ring in rings for v in ring.moving], *others))
    for i, ring in enumerate(rings):
        ring.moving = list(got[2 * i : 2 * i + 2])
        ring.step()
    return got[count] if len(others) == 1 else got[count:]


def crossed_blocks(own):
    share = [at_index(own, lax.axis_index("wsh") ^ r, 0) for r in range(own.shape[0])]
    return jnp.stack([share[0]] + [swap(share[r], r) for r in range(1, own.shape[0])])


def reduced(rows):
    return lax.psum_scatter(rows, "seq", scatter_dimension=0, tiled=True)


def local(
    hidden,
    teacher,
    cotangent,
    lengths,
    norm_gain,
    in_weight,
    conv_weight,
    conv_bias,
    x_weight,
    dt_weight,
    dt_bias,
    a_log,
    skip_gain,
    out_weight,
):
    me = lax.axis_index("wsh")
    place = lax.axis_index("seq")
    seqs = lax.axis_size("wsh")
    seq_count = lax.axis_size("seq")
    tokens, width = hidden.shape[1:]
    inner = out_weight.shape[0]
    depth = in_weight.shape[0]
    states = a_log.shape[0]
    rank = dt_weight.shape[0]
    taps = conv_weight.shape[0]
    rows = seqs * tokens

    def slots(pieces):
        return [at_index(pieces, me ^ r, 0) for r in range(seqs)]

    at = jnp.stack([place, me]).astype(jnp.int32)

    quarter = depth // 4
    half = quarter // 2
    part = place % 4

    def columns_from(start, ready):
        def block(r, first, size):
            return lax.dynamic_slice(ready, (first, start + (me ^ r) * inner), (size, inner))

        sent = [block(r, part * quarter, quarter) for r in (2, 3)]
        far = [swap(v, r) for v, r in zip(sent, (2, 3))]
        return far, [block(0, 0, depth), swap(block(1, 0, depth), 1)], sent

    def over_seq(far):
        return [seq_xor(v, bit) for bit in (1, 2) for v in far]

    def ends(by):
        return [seq_xor(v[:half], 1) for v in by[2:]] + [seq_xor(v[half:], 2) for v in by[:2]]

    x_far, x_near, x_sent = columns_from(0, in_weight)

    note = jnp.concatenate([norm_gain.astype(F32), lengths.astype(F32), jnp.zeros((127,), F32)])
    notes = jnp.stack(spread_out(tied(note, x_sent)))
    gain = jnp.concatenate(slots(notes[:, : norm_gain.shape[0]]))
    slot_lengths = notes[:, norm_gain.shape[0]]
    count = jnp.sum(jnp.minimum(slot_lengths, seq_count * tokens))
    positions = place * tokens + lax.iota(jnp.int32, tokens)
    valid = (positions[None, :].astype(F32) < slot_lengths[:, None]).astype(F32)
    halo_positions = place * tokens - HALO + lax.iota(jnp.int32, HALO + tokens)
    halo_valid = (halo_positions[None, :].astype(F32) < slot_lengths[:, None]).astype(F32)

    rows_in = hidden[0].astype(F32)
    scale = lax.rsqrt(jnp.mean(rows_in * rows_in, axis=1, keepdims=True) + NORM_EPS)
    normed_own = (rows_in * scale * gain).astype(BF16)
    before = shifted(normed_own[tokens - HALO :], 1)
    normed_own = tied(jnp.concatenate([before, normed_own], axis=0), x_far)
    normed_one, normed_two = swap(normed_own, 1), swap(normed_own, 2)
    x_by = over_seq(x_far)
    x_ends = ends(x_by)
    normed_two, x_ends = lax.optimization_barrier((normed_two, x_ends))
    normed = [normed_own, normed_one, normed_two, swap(normed_two, 1)]
    x_columns = join(at, [*x_near, *x_far, *x_by, *x_ends], width)
    z_far, z_near, _ = columns_from(seqs * inner, tied(in_weight, normed_two))
    normed = jnp.stack(normed)
    normed_tokens = normed[:, HALO:].reshape(rows, width)

    x_both = product(normed.reshape(seqs * (HALO + tokens), width), x_columns, PLAIN)
    x_in = (x_both.reshape(seqs, HALO + tokens, inner) * halo_valid[:, :, None]).astype(BF16)
    padded = x_in[:, HALO - (taps - 1) :].astype(F32)
    conv_f = conv_weight.astype(F32)
    conv_out = conv_bias.astype(F32) + sum(
        conv_f[tap] * padded[:, tap : tap + tokens] for tap in range(taps)
    )
    conv_out = conv_out.reshape(rows, inner)
    act = silu_value(conv_out).astype(BF16)
    proj = sum_all(tied(product(x_weight, act, COLS_LAST), z_far)).astype(BF16)
    dt_low = proj[:rank]
    bc = proj[rank:].astype(F32)
    step = jax.nn.softplus(product(dt_low, dt_weight, ROWS_FIRST) + dt_bias.astype(F32))
    log_rate = a_log.astype(F32)
    rate = -jnp.exp(log_rate) * LOG2E
    skip = skip_gain.astype(F32)[None]

    z_by = over_seq(tied(z_far, step))
    last_far, total_far = p1(2, step, act, bc, rate, tokens)
    z_by, last_far, total_far = lax.optimization_barrier((z_by, last_far, total_far))
    z_ends = ends(z_by)
    carry_far = Carry(total_far, last_far, rate, False)
    last_near, total_near = p1(0, tied(step, last_far), act, bc, rate, tokens)
    z_ends, last_near, total_near = carry_far.held(z_ends, last_near, total_near)
    carry_far.second()
    carry_near = Carry(total_near, last_near, rate, False)
    z_columns = join(at, [*z_near, *z_far, *z_by, *z_ends], width)
    z_part = product(normed_tokens, z_columns, PLAIN)
    z_part = carry_near.held(carry_far.held(z_part))
    carry_near.second()
    carry_far = carry_far.result()
    mixed_far, gated_far, starts_far = p2(2, step, act, z_part, bc, rate, skip, carry_far, tokens)
    mixed_far, gated_far, starts_far = carry_near.held(mixed_far, gated_far, starts_far)
    carry_near = carry_near.result()

    def parts(gated):
        return product(gated, out_weight, PLAIN).reshape(2, tokens, width)

    far = parts(gated_far)
    far = swap((far[0] + swap(far[1].astype(BF16), 1).astype(F32)).astype(BF16), 2)
    mixed_near, gated_near, starts_near = p2(0, step, act, z_part, bc, rate, skip, carry_near, tokens)
    far, gated_near = lax.optimization_barrier((far, gated_near))
    near = parts(gated_near)
    near = near[0] + swap(near[1].astype(BF16), 1).astype(F32)
    full = rows_in + near + far.astype(F32)
    own_valid = valid[0][:, None]
    miss = full - teacher[0].astype(F32)
    g_full = cotangent[0].astype(F32) + 2.0 / (width * count) * own_valid * miss
    g_own = g_full.astype(BF16)
    loss_part = jnp.sum(own_valid * miss * miss)

    g_one, g_two = swap(g_own, 1), swap(g_own, 2)
    g_branch_near = jnp.concatenate([g_own, g_one], axis=0)

    def into_mixer(g_branch, mixed, first):
        z = z_part[first * tokens : (first + 2) * tokens]
        g_gated = product(g_branch, out_weight, COLS_LAST)
        return g_gated * silu_value(z), (g_gated * mixed * silu_slope(z)).astype(BF16)

    g_mixed_near, g_z_near = into_mixer(g_branch_near, mixed_near, 0)
    first_near = b1(0, step, g_mixed_near, bc, rate, tokens)
    g_two, first_near = lax.optimization_barrier((g_two, first_near))
    back_near = Carry(total_near, first_near, rate, True)
    g_branch_far = jnp.concatenate([g_two, swap(g_two, 1)], axis=0)
    gated = jnp.concatenate([gated_near, gated_far], axis=0)
    out_grad = product(gated, jnp.concatenate([g_branch_near, g_branch_far], axis=0), ROWS_FIRST).astype(BF16)
    by_steps = seq_count == 8
    g_mixed_far, g_z_far = into_mixer(g_branch_far, mixed_far, 2)
    g_mixed_far, g_z_far = back_near.held(g_mixed_far, g_z_far)
    back_near.second()
    first_far = b1(2, step, g_mixed_far, bc, rate, tokens)
    first_far = back_near.held(first_far)
    back_near = back_near.result()
    back_far = Carry(total_far, first_far, rate, True)
    g_z = jnp.concatenate([g_z_near, g_z_far], axis=0)

    def in_shares(g, normed):
        return product(normed, g, ROWS_FIRST).astype(BF16).reshape(seqs, seq_count, depth // seq_count, g.shape[1])

    def way(v, d):
        wide = v.shape[-1] // 2
        return v[..., d * wide : (d + 1) * wide]

    def in_chunk(shares):
        return lambda d, q: at_index(way(shares, d), q, 1).reshape(width // seq_count, inner // 2)

    def in_between(own):
        return [crossed_blocks(v.reshape(seqs, -1, inner // 2)).reshape(v.shape) for v in own]

    out_own = reduced(out_grad)
    pair_near = (step, act, g_mixed_near, bc, rate, skip, starts_near, back_near, tokens)
    zero = b2(0, 1, None, *pair_near)
    zero = back_far.held(*zero)
    back_far.second()
    g_z = tied(g_z, zero)
    z_shares = jnp.swapaxes(in_shares(g_z, normed_tokens), 0, 1).reshape(width, inner)
    one = b2(1, 1, zero[:2], *pair_near)
    one = back_far.held(*one)
    back_far = back_far.result()
    z_shares, back_far = lax.optimization_barrier((z_shares, back_far))
    pair_far = (step, act, g_mixed_far, bc, rate, skip, starts_far, back_far, tokens)
    two = b2(2, 1, one[:2], *pair_far)
    out_own, *two = lax.optimization_barrier((out_own, *two))
    z_own = reduced(tied(z_shares, out_own))
    three = b2(3, 1, two[:2], *pair_far)
    far = [*three[:2], *[jnp.concatenate([v, w]) for v, w in zip(two[2:], three[2:])]]
    near = [jnp.concatenate([v, w]) for v, w in zip(zero[2:], one[2:])]
    g_pre, g_act_part = far[:2]
    g_b, g_c = [jnp.concatenate([near[i], far[2 + i]]).reshape(rows, states).T for i in (0, 1)]
    rate_sum, sums = [jnp.sum(near[i] + far[2 + i], axis=0) for i in (2, 3)]
    dt_bias_grad, skip_grad = jnp.sum(sums, axis=1)
    g_dt_low = product(dt_weight, g_pre, COLS_LAST)
    g_proj = sum_all(
        jnp.concatenate([g_dt_low, g_b, g_c], axis=0)
    ).astype(BF16)
    g_act = g_act_part + product(g_proj, x_weight, ROWS_FIRST)
    g_conv = (g_act * silu_slope(conv_out)).reshape(seqs, tokens, inner)
    g_padded = jnp.pad(g_conv, ((0, 0), (HALO, taps - 1), (0, 0)))
    g_x = sum(
        conv_f[tap] * g_padded[:, taps - 1 - tap : taps - 1 - tap + HALO + tokens] for tap in range(taps)
    )
    g_x = (g_x * halo_valid[:, :, None]).astype(BF16)
    conv_grad = [jnp.sum(g_conv * padded[:, tap : tap + tokens], axis=(0, 1)) for tap in range(taps)]
    small = [
        product(g_proj, act, PLAIN),
        product(dt_low, g_pre, PLAIN),
        rate_sum * (rate * LN2),
        jnp.stack(conv_grad),
        jnp.sum(g_conv, axis=(0, 1))[None],
        dt_bias_grad[None],
        skip_grad[None],
    ]
    cut = [0]
    for piece in small:
        cut.append(cut[-1] + piece.shape[0])
    lines = 16 * seq_count
    small.append(jnp.zeros((-cut[-1] % lines, inner), F32))
    small = jnp.concatenate(small, axis=0)
    normed_all = normed.reshape(seqs * (HALO + tokens), width)
    g_x_all = g_x.reshape(seqs * (HALO + tokens), inner)
    if by_steps:
        x_shares = in_shares(g_x_all, normed_all)
        small_shares = small.astype(BF16).reshape(seq_count, -1, inner)
        z_own, x_shares, small_shares, g_x = lax.optimization_barrier((z_own, x_shares, small_shares, g_x))
        large = width // seq_count
        chunk_of = in_chunk(x_shares)

        def x_chunk(d, q):
            return jnp.concatenate([chunk_of(d, q), at_index(way(small_shares, d), q, 0)], axis=0)

        def x_between(own):
            return [jnp.concatenate([x, v[large:]], axis=0) for x, v in zip(in_between([v[:large] for v in own]), own)]

        x_ring = Ring(x_chunk, x_between)
        out_ring = Ring(None, None, [way(out_own, d) for d in range(2)])
        z_row = crossed_blocks(z_own.reshape(seqs, -1, inner)).reshape(-1, inner)
        rings = [x_ring, out_ring]
        z_row, g_x = advance(rings, z_row, g_x)
        z_ring = Ring(None, None, [way(z_row, d) for d in range(2)])
        rings.append(z_ring)
    after = shifted(g_x[:, HALO - (taps - 1) : HALO], -1)
    g_z = tied(g_z, g_x)

    def to_normed(g, columns, slot):
        return product(g[slot * tokens : (slot + 1) * tokens], columns, COLS_LAST)

    def advanced(*v):
        if by_steps:
            return advance([ring for ring in rings if not ring.done()], *v)
        return v[0] if len(v) == 1 else v

    normed_1, normed_3 = advanced(to_normed(g_z, z_columns, 1), to_normed(g_z, z_columns, 3))
    normed_2, after = advanced(to_normed(g_z, z_columns, 2), after)
    fixed = jnp.pad(after, ((0, 0), (tokens - (taps - 1), 0), (0, 0)))
    g_x = advanced((g_x[:, HALO:] + fixed).reshape(rows, inner))
    normed_1 += to_normed(g_x, x_columns, 1)
    normed_3 += to_normed(g_x, x_columns, 3)
    normed_1, normed_3 = advanced(normed_1.astype(BF16), normed_3.astype(BF16))
    got1, got3 = swap((normed_1, normed_3), 1)
    got1, got3, normed_2 = advanced(got1, got3, normed_2 + to_normed(g_x, x_columns, 2))
    other = swap((normed_2 + got3.astype(F32)).astype(BF16), 2)
    normed_0 = advanced(to_normed(g_z, z_columns, 0))
    normed_0 = advanced(normed_0 + to_normed(g_x, x_columns, 0) + got1.astype(F32))
    if by_steps:
        other = advanced(other)
    g_normed = normed_0 + other.astype(F32)
    gain_part = jnp.sum(g_normed * rows_in * scale, axis=0)
    tail = jnp.concatenate([gain_part, jnp.full((128,), loss_part)])
    if by_steps:
        where = jnp.stack([me] + ring_order()).astype(jnp.int32)
        out_is = partial(settle, where, out_ring.result(), out_weight.shape, 1, width)
        z_is = partial(settle, where, z_ring.result(), in_weight.shape, seqs, inner, half=1)
        assert out_ring.done() and z_ring.done()
        tail, out_owned = advanced(tail + seq_xor(tail, 1), out_is(part=0)[0])
        tail, out_owned = advanced(tail + seq_xor(tail, 2), out_is(part=1, filled=out_owned)[0])
        tail, in_owned = advanced(tail + seq_xor(tail, 4), z_is(part=0)[0])
    else:
        tail = lax.psum(tail, "seq")
    gain_share = slots(tail[:width].reshape(seqs, -1))
    gain_grad = gain_share[0] + sum(swap(gain_share[r], r) for r in range(1, seqs))
    loss_sum = tail[width:] + swap(tail[width:], 1)
    loss = (loss_sum + swap(loss_sum, 2))[0] / (width * count)
    if by_steps:
        gain_grad, loss, in_owned = advanced(gain_grad, loss, z_is(part=1, filled=in_owned)[0])
        while not x_ring.done():
            in_owned = advanced(in_owned)
        in_owned, small = settle(
            where, x_ring.result(), in_weight.shape, seqs, inner, filled=in_owned, extra=small.shape[0]
        )
    if not by_steps:
        x_shares = jnp.swapaxes(in_shares(g_x_all, normed_all), 0, 1)
        x_row = crossed_blocks(reduced(x_shares.reshape(width, inner)).reshape(seqs, -1, inner))
        x_owned = lax.all_gather(jnp.concatenate(slots(x_row), axis=1), "seq", axis=0, tiled=True)
        small = lax.psum(small, "seq")
        out_owned = lax.all_gather(out_own, "seq", axis=0, tiled=True)
        out_owned = spread_rows([out_owned], out_weight.shape)
        in_owned = spread_rows([x_owned], in_weight.shape)
        z_row = crossed_blocks(z_own.reshape(seqs, -1, inner))
        z_owned = lax.all_gather(jnp.concatenate(slots(z_row), axis=1), "seq", axis=0, tiled=True)
        in_owned = spread_rows([z_owned], in_weight.shape, 1, in_owned)
    x_grad, dt_grad, log_rate_grad, conv_grad, conv_bias_grad, dt_bias_grad, skip_grad = cut_rows(small, cut)
    weighted = g_normed * gain
    g_rows = (
        g_full
        + scale * weighted
        - rows_in * scale * scale * scale * jnp.mean(weighted * rows_in, axis=1, keepdims=True)
    )
    return (
        full[None].astype(BF16),
        loss,
        g_rows[None].astype(BF16),
        gain_grad,
        in_owned,
        conv_grad,
        conv_bias_grad[0],
        x_grad,
        dt_grad,
        dt_bias_grad[0],
        log_rate_grad,
        skip_grad[0],
        out_owned,
    )


def solution(mesh):
    rows = P("wsh", "seq", None)
    first, second = P("wsh", None), P(None, "wsh")
    one = P("wsh")
    return jax.shard_map(
        local,
        mesh=mesh,
        in_specs=(
            rows, rows, rows, one, one, first, second, one, second, second, one, second, one, first,
        ),
        out_specs=(
            rows, P(), rows, one, first, second, one, second, second, one, second, one, first,
        ),
        check_vma=False,
    )
```

```python
from functools import partial

import jax
import jax.numpy as jnp
from jax import lax
from jax.experimental import pallas as pl
from jax.experimental.pallas import tpu as pltpu
from jax.sharding import PartitionSpec as P

F32 = jnp.float32
BF16 = jnp.bfloat16
NORM_EPS = 1e-05
LOG2E = 1.4426950408889634
LN2 = 0.6931471805599453
GROUP = 8
CHUNK = 32
HALO = 16
VMEM_LIMIT = 56 * 1024 * 1024
ROWS_FIRST = (((0,), (0,)), ((), ()))
COLS_LAST = (((1,), (1,)), ((), ()))
PLAIN = (((1,), (0,)), ((), ()))


def product(left, right, dims):
    return lax.dot_general(left, right, dims, preferred_element_type=F32)


def silu_value(v):
    return v * jax.nn.sigmoid(v)


def silu_slope(v):
    sigma = jax.nn.sigmoid(v)
    return sigma * (1.0 + v * (1.0 - sigma))


def kernel_params():
    return pltpu.CompilerParams(vmem_limit_bytes=VMEM_LIMIT)


def cost(microseconds):
    return pl.CostEstimate(flops=int(microseconds * 1e9), bytes_accessed=0, transcendentals=0)


def widen(bc_ref, row, size, rep_ref):
    ones = jnp.ones((128, 128), BF16)
    lane = lax.broadcasted_iota(jnp.int32, (size, 128), 1)
    part = 32

    def block(i, _):
        t0 = pl.multiple_of(i * 128, 128)
        x = bc_ref[row : row + size, pl.ds(t0, 128)]
        for j in range(0, 128, part):
            picked = jnp.concatenate([jnp.where(lane == k, x, 0.0) for k in range(j, j + part)], axis=0)
            wide = jnp.dot(picked.astype(BF16), ones, preferred_element_type=F32)
            rep_ref[pl.ds(t0 + j, part)] = wide.reshape(part, size, 128)
        return 0

    lax.fori_loop(0, bc_ref.shape[1] // 128, block, 0)


def tiled(x, width):
    return jnp.concatenate([x]*(width//128), axis=1)

def put_fold(fold_ref,k,v):
    for i in range(v.shape[1]//128):
        fold_ref[i,8*k:8*k+8,:]=v[:,128*i:128*i+128]

def get_fold(fold_ref):
    def tree(x):
        while len(x)>1: x=[a+b for a,b in zip(x[::2],x[1::2])]
        return x[0]
    return jnp.concatenate([tree([fold_ref[i,pl.ds(r,GROUP,stride=8),:] for r in range(8)]) for i in range(fold_ref.shape[0])],axis=1)

def p1_kernel(step_ref, act_ref, bc_ref, rate_ref, last_ref, total_ref, dx_ref, brep_ref, *, eb, n):
    widen(bc_ref,0,n,brep_ref)
    step=step_ref[...]
    dx_ref[...]=step*act_ref[...].astype(F32)
    total_ref[0]=jnp.sum(step,axis=0,keepdims=True)
    tokens,width=step_ref.shape
    for e in range(0,width,eb):
        sl=slice(e,e+eb)
        rate=rate_ref[:,sl]
        def group(g,h):
            base=pl.multiple_of(g*GROUP,GROUP)
            s8=step_ref[pl.ds(base,GROUP),sl]
            x8=dx_ref[pl.ds(base,GROUP),sl]
            for k in range(GROUP):
                d=jnp.exp2(rate*s8[k:k+1])
                h=d*h+tiled(brep_ref[base+k],eb)*x8[k:k+1]
            return h
        last_ref[0,:,sl]=lax.fori_loop(0,tokens//GROUP,group,jnp.zeros((n,eb),F32))

def p1(first, step, act, bc, rate, tokens, eb=512):
    width = step.shape[1]
    n = rate.shape[0]
    blk = pl.BlockSpec((tokens, width), lambda s: (first + s, 0))
    return pl.pallas_call(
        partial(p1_kernel, eb=eb, n=n),
        grid=(2,),
        in_specs=[
            blk,
            blk,
            pl.BlockSpec((bc.shape[0], tokens), lambda s: (0, first + s)),
            pl.BlockSpec((n, width), lambda s: (0, 0)),
        ],
        out_specs=[
            pl.BlockSpec((1, n, width), lambda s: (s, 0, 0)),
            pl.BlockSpec((1, 1, width), lambda s: (s, 0, 0)),
        ],
        out_shape=[jax.ShapeDtypeStruct((2, n, width), F32), jax.ShapeDtypeStruct((2, 1, width), F32)],
        scratch_shapes=[pltpu.VMEM((tokens, width), F32), pltpu.VMEM((tokens, n, 128), F32)],
        cost_estimate=cost(9),
        compiler_params=kernel_params(),
    )(step, act, bc, rate)


def p2_kernel(step_ref, act_ref, z_ref, bc_ref, rate_ref, skip_ref, carry_ref, mixed_ref, gated_ref, starts_ref, dx_ref, fold_ref, brep_ref, crep_ref, *, eb, n):
    widen(bc_ref,0,n,brep_ref)
    widen(bc_ref,n,n,crep_ref)
    dx_ref[...]=step_ref[...]*act_ref[...].astype(F32)
    tokens,width=step_ref.shape
    for e in range(0,width,eb):
        sl=slice(e,e+eb)
        rate=rate_ref[:,sl]
        def chunk(c,h):
            starts_ref[0,c,:,sl]=h
            def group(j,h):
                g=c*(CHUNK//GROUP)+j
                base=pl.multiple_of(g*GROUP,GROUP)
                s8=step_ref[pl.ds(base,GROUP),sl]
                x8=dx_ref[pl.ds(base,GROUP),sl]
                for k in range(GROUP):
                    d=jnp.exp2(rate*s8[k:k+1])
                    h=d*h+tiled(brep_ref[base+k],eb)*x8[k:k+1]
                    p=tiled(crep_ref[base+k],eb)*h
                    put_fold(fold_ref,k,sum(p[8*i:8*i+8] for i in range(n//8)))
                mixed_ref[pl.ds(base,GROUP),sl]=get_fold(fold_ref)
                return h
            return lax.fori_loop(0,CHUNK//GROUP,group,h)
        lax.fori_loop(0,tokens//CHUNK,chunk,carry_ref[0,:,sl])
    def gate(i,_):
        rows=pl.ds(pl.multiple_of(i*16,16),16)
        m=mixed_ref[rows,:]+skip_ref[...]*act_ref[rows,:].astype(F32)
        mixed_ref[rows,:]=m
        z=z_ref[rows,:]
        gated_ref[rows,:]=(m*(z*jax.nn.sigmoid(z))).astype(BF16)
        return 0
    lax.fori_loop(0,tokens//16,gate,0)

def p2(first, step, act, z, bc, rate, skip, carry, tokens, eb=512):
    width = step.shape[1]
    n = rate.shape[0]
    nch = tokens // CHUNK
    blk = pl.BlockSpec((tokens, width), lambda s: (first + s, 0))
    out = pl.BlockSpec((tokens, width), lambda s: (s, 0))
    rep = pltpu.VMEM((tokens, n, 128), F32)
    return pl.pallas_call(
        partial(p2_kernel, eb=eb, n=n),
        grid=(2,),
        in_specs=[
            blk,
            blk,
            blk,
            pl.BlockSpec((bc.shape[0], tokens), lambda s: (0, first + s)),
            pl.BlockSpec((n, width), lambda s: (0, 0)),
            pl.BlockSpec((1, width), lambda s: (0, 0)),
            pl.BlockSpec((1, n, width), lambda s: (s, 0, 0)),
        ],
        out_specs=[out, out, pl.BlockSpec((1, nch, n, width), lambda s: (s, 0, 0, 0))],
        out_shape=[
            jax.ShapeDtypeStruct((2 * tokens, width), F32),
            jax.ShapeDtypeStruct((2 * tokens, width), BF16),
            jax.ShapeDtypeStruct((2, nch, n, width), F32),
        ],
        scratch_shapes=[pltpu.VMEM((tokens, width), F32), pltpu.VMEM((eb // 128, 64, 128), F32), rep, rep],
        cost_estimate=cost(16),
        compiler_params=kernel_params(),
    )(step, act, z, bc, rate, skip, carry)


def b1_kernel(step_ref, dy_ref, bc_ref, rate_ref, first_ref, crep_ref, *, eb, n):
    widen(bc_ref,n,n,crep_ref)
    tokens,width=step_ref.shape
    for e in range(0,width,eb):
        sl=slice(e,e+eb)
        rate=rate_ref[:,sl]
        def group(j,h):
            g=tokens//GROUP-1-j
            base=pl.multiple_of(g*GROUP,GROUP)
            s8=step_ref[pl.ds(base,GROUP),sl]
            y8=dy_ref[pl.ds(base,GROUP),sl]
            for k in reversed(range(GROUP)):
                h=jnp.exp2(rate*s8[k:k+1])*(h+tiled(crep_ref[base+k],eb)*y8[k:k+1])
            return h
        first_ref[0,:,sl]=lax.fori_loop(0,tokens//GROUP,group,jnp.zeros((n,eb),F32))

def b1(first, step, dy, bc, rate, tokens, eb=512):
    width = step.shape[1]
    n = rate.shape[0]
    return pl.pallas_call(
        partial(b1_kernel, eb=eb, n=n),
        grid=(2,),
        in_specs=[
            pl.BlockSpec((tokens, width), lambda s: (first + s, 0)),
            pl.BlockSpec((tokens, width), lambda s: (s, 0)),
            pl.BlockSpec((bc.shape[0], tokens), lambda s: (0, first + s)),
            pl.BlockSpec((n, width), lambda s: (0, 0)),
        ],
        out_specs=pl.BlockSpec((1, n, width), lambda s: (s, 0, 0)),
        out_shape=jax.ShapeDtypeStruct((2, n, width), F32),
        scratch_shapes=[pltpu.VMEM((tokens, n, 128), F32)],
        cost_estimate=cost(9),
        compiler_params=kernel_params(),
    )(step, dy, bc, rate)


def one_less_exp(s):
    return jnp.where(s<0.01, s*(1.0-s*(0.5-s*(1.0/6.0))), 1.0-jnp.exp(-s))

def b2_kernel(step_ref, act_ref, dy_ref, bc_ref, rate_ref, skip_ref, starts_ref, carry_ref, *refs, eb, n):
    (gpre_ref, gact_ref, gb_ref, gc_ref, alog_ref, dtb_ref, dx_ref, prev_ref, dec_ref, folda_ref, folds_ref,
     pb_ref, pc_ref, g_ref, brep_ref, crep_ref) = refs[-16:]
    widen(bc_ref,0,n,brep_ref)
    widen(bc_ref,n,n,crep_ref)
    tokens,width=step_ref.shape
    nch=tokens//CHUNK; per=CHUNK//GROUP
    dx_ref[...]=step_ref[...]*act_ref[...].astype(F32)
    g_ref[...]=carry_ref[0]
    alog_ref[...]=jnp.zeros_like(alog_ref)
    ones=jnp.ones((8,128),F32)
    def chunk(cc,_):
        c=nch-1-cc
        for e in range(0,width,eb):
            sl=slice(e,e+eb)
            rate=rate_ref[:,sl]
            def redo(j,h):
                g=c*per+j
                base=pl.multiple_of(g*GROUP,GROUP)
                s8=step_ref[pl.ds(base,GROUP),sl]
                x8=dx_ref[pl.ds(base,GROUP),sl]
                for k in range(GROUP):
                    d=jnp.exp2(rate*s8[k:k+1])
                    prev_ref[j*GROUP+k]=h
                    dec_ref[j*GROUP+k]=d
                    h=d*h+tiled(brep_ref[base+k],eb)*x8[k:k+1]
                return h
            last=lax.fori_loop(0,per,redo,starts_ref[0,c,:,sl])
            def back(jj,carry):
                h,alog,after=carry
                j=per-1-jj
                g=c*per+j
                base=pl.multiple_of(g*GROUP,GROUP)
                s8=step_ref[pl.ds(base,GROUP),sl]
                x8=dx_ref[pl.ds(base,GROUP),sl]
                y8=dy_ref[pl.ds(base,GROUP),sl]
                for k in reversed(range(GROUP)):
                    s=s8[k:k+1]
                    g_state=tiled(crep_ref[base+k],eb)*y8[k:k+1]+h
                    prev=prev_ref[j*GROUP+k]
                    pc=after*y8[k:k+1]
                    pb=g_state*x8[k:k+1]
                    al=g_state*tiled(brep_ref[base+k],eb)
                    h=g_state*dec_ref[j*GROUP+k]
                    q=h*prev
                    alog=alog+q*s
                    qs=q*rate
                    pcs=sum(pc[:,i:i+128] for i in range(0,eb,128))
                    pbs=sum(pb[:,i:i+128] for i in range(0,eb,128))
                    rows=pl.ds(pl.multiple_of((j*GROUP+k)*n,n),n)
                    if e==0:
                        pc_ref[rows,:]=pcs; pb_ref[rows,:]=pbs
                    else:
                        pc_ref[rows,:]+=pcs; pb_ref[rows,:]+=pbs
                    put_fold(folda_ref,k,sum(al[8*i:8*i+8] for i in range(n//8)))
                    put_fold(folds_ref,k,sum(qs[8*i:8*i+8] for i in range(n//8)))
                    after=prev
                gact_ref[pl.ds(base,GROUP),sl]=get_fold(folda_ref)
                dx_ref[pl.ds(base,GROUP),sl]=get_fold(folds_ref)
                return h,alog,after
            h,alog,_u=lax.fori_loop(0,per,back,(g_ref[:,sl],jnp.zeros((n,eb),F32),last))
            g_ref[:,sl]=h
            alog_ref[0,:,sl]+=alog
        for j in range(per):
            part=pb_ref[j*128:(j+1)*128,:]
            gb_ref[0,pl.ds(c*per+j,1),:]=lax.dot_general(ones,part,(((1,),(1,)),((),())),precision=lax.Precision.HIGHEST,preferred_element_type=F32)[0:1]
            part=pc_ref[j*128:(j+1)*128,:]
            gc_ref[0,pl.ds(c*per+j,1),:]=lax.dot_general(ones,part,(((1,),(1,)),((),())),precision=lax.Precision.HIGHEST,preferred_element_type=F32)[0:1]
        return 0
    lax.fori_loop(0,nch,chunk,0)
    def finish(i,acc):
        rows=pl.ds(pl.multiple_of(i*16,16),16)
        s=step_ref[rows,:]; along=gact_ref[rows,:]
        a=act_ref[rows,:].astype(F32)
        garg=(dx_ref[rows,:]*LN2+a*along)*one_less_exp(s)
        gpre_ref[rows,:]=garg.astype(BF16)
        dy=dy_ref[rows,:]
        gact_ref[rows,:]=dy*skip_ref[...]+s*along
        return acc[0]+jnp.sum(garg.reshape(2,8,width),axis=0), acc[1]+jnp.sum((dy*a).reshape(2,8,width),axis=0)
    zero=jnp.zeros((8,width),F32)
    acc=lax.fori_loop(0,tokens//16,finish,(zero,zero))
    dtb_ref[0,0]=acc[0]
    dtb_ref[0,1]=acc[1]

def b2(first, count, filled, step, act, dy, bc, rate, skip, starts, carry, tokens, eb=512):
    base = first % 2
    rows, width = step.shape
    n = rate.shape[0]
    nch = tokens // CHUNK
    blk = pl.BlockSpec((tokens, width), lambda i: (first + i, 0))
    full = lambda shape: pl.BlockSpec(shape, lambda i: (0,) * len(shape))
    own = lambda shape: pl.BlockSpec((1, *shape[1:]), lambda i: (i,) + (0,) * (len(shape) - 1))
    red = (count, tokens // GROUP, 128)
    rep = pltpu.VMEM((tokens, n, 128), F32)
    held = pltpu.VMEM((CHUNK, n, eb), F32)
    fold = pltpu.VMEM((eb // 128, 64, 128), F32)
    part = pltpu.VMEM((CHUNK * n, 128), F32)
    extra = () if filled is None else tuple(filled)
    return pl.pallas_call(
        partial(b2_kernel, eb=eb, n=n),
        grid=(count,),
        in_specs=[
            blk,
            blk,
            pl.BlockSpec((tokens, width), lambda i: (base + i, 0)),
            pl.BlockSpec((bc.shape[0], tokens), lambda i: (0, first + i)),
            full((n, width)),
            full((1, width)),
            pl.BlockSpec((1, nch, n, width), lambda i: (base + i, 0, 0, 0)),
            pl.BlockSpec((1, n, width), lambda i: (base + i, 0, 0)),
        ]
        + [pl.BlockSpec(memory_space=pl.ANY)] * len(extra),
        out_specs=[blk, blk, own(red), own(red), own((count, n, width)), own((count, 2, 8, width))],
        out_shape=[
            jax.ShapeDtypeStruct((rows, width), BF16),
            jax.ShapeDtypeStruct((rows, width), F32),
            jax.ShapeDtypeStruct(red, F32),
            jax.ShapeDtypeStruct(red, F32),
            jax.ShapeDtypeStruct((count, n, width), F32),
            jax.ShapeDtypeStruct((count, 2, 8, width), F32),
        ],
        scratch_shapes=[
            pltpu.VMEM((tokens, width), F32),
            held,
            held,
            fold,
            fold,
            part,
            part,
            pltpu.VMEM((n, width), F32),
            rep,
            rep,
        ],
        input_output_aliases={8: 0, 9: 1} if extra else {},
        cost_estimate=cost(25 * count),
        compiler_params=kernel_params(),
    )(step, act, dy, bc, rate, skip, starts, carry, *extra)


def settle_kernel(at_ref, *refs, steps, base, blocks, cols, extra):
    out_ref = refs[-2] if extra else refs[-1]
    rows = out_ref.shape[0]
    i = base + pl.program_id(0)
    for d in range(2):
        for k in range(steps):
            ref = refs[d * steps + k]
            wide = ref.shape[1]

            @pl.when(at_ref[1 + d * steps + i] == k)
            def _():
                for r in range(blocks):
                    start = d * wide
                    if blocks > 1:
                        start = pl.multiple_of((at_ref[0] ^ r) * cols + start, 128)
                    out_ref[:, pl.ds(start, wide)] = ref[r * rows : (r + 1) * rows, :].astype(F32)
                if extra:
                    refs[-1][:, d * wide : (d + 1) * wide] = ref[blocks * rows :, :].astype(F32)


def settle(at, both, shape, blocks, cols, half=0, filled=None, extra=0, part=None):
    steps = len(both[0])
    rows, wide = both[0][0].shape
    piece = (rows - extra // steps) // blocks
    span = blocks * cols if blocks > 1 else 2 * wide
    given = [] if filled is None else [filled]
    count, base = (steps, 0) if part is None else (steps // 2, part * steps // 2)
    out_specs = [pl.BlockSpec((piece, span), lambda i, at_ref: (base + i, half))]
    out_shape = [jax.ShapeDtypeStruct(shape, F32)]
    if extra:
        out_specs.append(pl.BlockSpec((extra // steps, 2 * wide), lambda i, at_ref: (base + i, 0)))
        out_shape.append(jax.ShapeDtypeStruct((extra, 2 * wide), F32))
    whole = pl.BlockSpec((rows, wide), lambda i, at_ref: (0, 0))
    return pl.pallas_call(
        partial(settle_kernel, steps=steps, base=base, blocks=blocks, cols=cols, extra=extra),
        grid_spec=pltpu.PrefetchScalarGridSpec(
            num_scalar_prefetch=1,
            grid=(count,),
            in_specs=[whole] * (2 * steps) + [pl.BlockSpec(memory_space=pl.ANY)] * len(given),
            out_specs=out_specs,
        ),
        out_shape=out_shape,
        input_output_aliases={1 + 2 * steps: 0} if given else {},
        cost_estimate=cost(7 if part is None else 4),
        compiler_params=kernel_params(),
    )(at, *both[0], *both[1], *given)


def cut_rows_kernel(v_ref, *out_refs, cut):
    for ref, first in zip(out_refs, cut):
        ref[...] = v_ref[first : first + ref.shape[0], :]


def cut_rows(v, cut):
    whole = pl.BlockSpec(memory_space=pltpu.VMEM)
    sizes = [b - a for a, b in zip(cut, cut[1:])]
    return pl.pallas_call(
        partial(cut_rows_kernel, cut=cut),
        in_specs=[whole],
        out_specs=[whole] * len(sizes),
        out_shape=[jax.ShapeDtypeStruct((size, v.shape[1]), F32) for size in sizes],
        cost_estimate=cost(2),
        compiler_params=kernel_params(),
    )(v)


def spread_rows_kernel(*refs, count):
    out_ref = refs[-1]
    wide = refs[0].shape[1]
    for h in range(count):
        out_ref[:, h * wide : (h + 1) * wide] = refs[h][...].astype(F32)


def spread_rows(parts, shape, half=0, filled=None, part=None):
    rows, wide = parts[0].shape
    given = [] if filled is None else [filled]
    count, base = (8, 0) if part is None else (4, 4 * part)
    return pl.pallas_call(
        partial(spread_rows_kernel, count=len(parts)),
        grid=(count,),
        in_specs=[pl.BlockSpec((rows // 8, wide), lambda i: (base + i, 0))] * len(parts)
        + [pl.BlockSpec(memory_space=pl.ANY)] * len(given),
        out_specs=pl.BlockSpec((rows // 8, wide * len(parts)), lambda i: (base + i, half)),
        out_shape=jax.ShapeDtypeStruct(shape, F32),
        input_output_aliases={len(parts): 0} if given else {},
        cost_estimate=cost(4),
        compiler_params=kernel_params(),
    )(*parts, *given)


def join_kernel(at_ref, *refs):
    part, me = at_ref[0] % 4, at_ref[1]
    near_ref, next_ref, *far_refs, out_ref = refs
    depth = near_ref.shape[0]
    quarter = depth // 4
    half = quarter // 2

    def put(row, ref):
        out_ref[pl.ds(pl.multiple_of(row, half), ref.shape[0]), :] = ref[...]

    put(me * depth, near_ref)
    put((me ^ 1) * depth, next_ref)
    for k in range(2):
        start = (me ^ (2 + k)) * depth
        own, one, two, end, tail = far_refs[k::2]
        put(start + part * quarter, own)
        put(start + (part ^ 1) * quarter, one)
        put(start + (part ^ 2) * quarter, two)
        put(start + (part ^ 3) * quarter, end)
        put(start + (part ^ 3) * quarter + half, tail)


def join(at, pieces, rows):
    wide = pieces[0].shape[1]
    return pl.pallas_call(
        join_kernel,
        in_specs=[pl.BlockSpec(memory_space=pltpu.SMEM)] + [pl.BlockSpec(memory_space=pltpu.VMEM)] * len(pieces),
        out_specs=pl.BlockSpec(memory_space=pltpu.VMEM),
        out_shape=jax.ShapeDtypeStruct((rows, wide), BF16),
        cost_estimate=cost(4),
        compiler_params=kernel_params(),
    )(at, *pieces)


def swap(v, bit):
    return jax.tree.map(
        lambda a: lax.ppermute(a, "wsh", [(i, i ^ bit) for i in range(lax.axis_size("wsh"))]), v
    )


def shifted(v, distance):
    count = lax.axis_size("seq")
    route = [(i - distance, i) for i in range(count) if 0 <= i - distance < count]
    return jax.tree.map(lambda a: lax.ppermute(a, "seq", route), v)


def spread_out(v):
    one = swap(v, 1)
    two = swap(v, 2)
    return [v, one, two, swap(two, 1)]


def sum_to_owner(parts, own_cast=BF16):
    got1, got3 = swap((parts[1].astype(own_cast), parts[3].astype(own_cast)), 1)
    mine = parts[0] + got1.astype(F32)
    other = (parts[2] + got3.astype(F32)).astype(own_cast)
    return mine + swap(other, 2).astype(F32)


def crossed(v, bit):
    got = jnp.split(swap(v, bit), lax.axis_size("wsh"), axis=1)
    return jnp.concatenate([got[r ^ bit] for r in range(len(got))], axis=1)


def sum_all(v):
    v = v + crossed(v, 1)
    return v + crossed(v.astype(BF16), 2).astype(F32)


def hi_lo(v):
    hi = v.astype(BF16)
    return [hi, (v - hi.astype(F32)).astype(BF16)]


def carried_far(total, state, rate, reverse):
    count = lax.axis_size("seq")
    sign = -1 if reverse else 1
    total, state = shifted((total, state), sign)
    hop = 1
    while hop < count:
        got_total, got_state = shifted((total, state), sign * hop)
        state = state + jnp.exp2(rate[None] * total) * got_state
        total = total + got_total
        hop *= 2
    return state


class Carry:
    def __init__(self, total, state, rate, reverse):
        self.total, self.rate, self.reverse = total, rate, reverse
        self.near = lax.axis_size("seq") == 8
        if self.near:
            self.state = state
            self.moved = [seq_xor(self.packed(total, state), 1)]
        else:
            self.moved = [carried_far(total, state, rate, reverse)]

    def held(self, *others):
        count = len(self.moved)
        got = lax.optimization_barrier((*self.moved, *others))
        self.moved = list(got[:count])
        return got[count] if len(others) == 1 else got[count:]

    def packed(self, t, s):
        return jnp.concatenate([s.astype(BF16)] + hi_lo(t), axis=1)

    def opened(self, v):
        v = v.astype(F32)
        n = self.rate.shape[0]
        return v[:, n : n + 1] + v[:, n + 1 : n + 2], v[:, :n]

    def fall(self, t):
        return jnp.exp2(self.rate[None] * t)

    def second(self):
        if not self.near:
            return self
        place = lax.axis_index("seq")
        self.other_total, self.other_state = self.opened(self.moved[0])
        self.late = (place % 2 == 1) != self.reverse
        early_state = jnp.where(self.late, self.other_state, self.state)
        late_state = jnp.where(self.late, self.state, self.other_state)
        late_total = jnp.where(self.late, self.total, self.other_total)
        message = self.packed(self.total + self.other_total, self.fall(late_total) * early_state + late_state)
        sign = -1 if self.reverse else 1
        self.moved = [shifted(message, sign * 2 * k) for k in range(1, 4)]
        return self

    def result(self):
        if not self.near:
            return self.moved[0]
        got = [self.opened(v) for v in self.moved]
        carry = got[-1][1]
        for t, s in reversed(got[:-1]):
            carry = s + self.fall(t) * carry
        return jnp.where(self.late, self.fall(self.other_total) * carry + self.other_state, carry)


def seq_xor(v, bits):
    return lax.ppermute(v, "seq", [(i, i ^ bits) for i in range(lax.axis_size("seq"))])


def tied(v, *before):
    return lax.optimization_barrier((v, before))[0]


def at_index(v, index, axis):
    return lax.dynamic_index_in_dim(v, index, axis, False)


RING = (0, 2, 4, 6, 7, 5, 3, 1)


def ring_place():
    q = lax.axis_index("seq")
    return jnp.where(q % 2 == 0, q // 2, len(RING) - 1 - q // 2)


def ring_device(place):
    place = place % len(RING)
    return jnp.where(place < len(RING) // 2, 2 * place, 2 * len(RING) - 1 - 2 * place)


def ring_order():
    places = [RING.index(q) for q in range(len(RING))]
    p = ring_place()
    return [(p - k) % len(RING) for k in places] + [(k - p) % len(RING) for k in places]


class Ring:
    def __init__(self, share, between, own=None):
        self.share, self.between = share, between
        self.count, self.steps = len(RING), 0
        self.place = ring_place()
        if own is None:
            self.send([self.chunk(d, 1) for d in range(2)])
        else:
            self.steps = self.count - 1
            self.rounds = [[v] for v in own]
            self.send(own)

    def chunk(self, d, k):
        return self.share(d, ring_device(self.place + (k if d else self.count - k)))

    def send(self, held):
        self.steps += 1
        self.moving = []
        for d in range(2):
            route = [(RING[k], RING[(k + (-1 if d else 1)) % self.count]) for k in range(self.count)]
            self.moving.append(lax.ppermute(held[d], "seq", route))

    def step(self):
        k = self.steps + 1
        if k < self.count:
            self.send([self.added(d, k) for d in range(2)])
        elif k == self.count:
            own = self.between([self.added(d, k) for d in range(2)])
            self.rounds = [[v] for v in own]
            self.send(own)
        else:
            for d in range(2):
                self.rounds[d].append(self.moving[d])
            if k < 2 * self.count - 1:
                self.send(self.moving)

    def added(self, d, k):
        return (self.moving[d].astype(F32) + self.chunk(d, k).astype(F32)).astype(BF16)

    def result(self):
        return self.rounds

    def done(self):
        return self.steps >= self.count and len(self.rounds[0]) == self.count


def advance(rings, *others):
    count = 2 * len(rings)
    got = lax.optimization_barrier((*[v for ring in rings for v in ring.moving], *others))
    for i, ring in enumerate(rings):
        ring.moving = list(got[2 * i : 2 * i + 2])
        ring.step()
    return got[count] if len(others) == 1 else got[count:]


def crossed_blocks(own):
    share = [at_index(own, lax.axis_index("wsh") ^ r, 0) for r in range(own.shape[0])]
    return jnp.stack([share[0]] + [swap(share[r], r) for r in range(1, own.shape[0])])


def reduced(rows):
    return lax.psum_scatter(rows, "seq", scatter_dimension=0, tiled=True)


def local(
    hidden,
    teacher,
    cotangent,
    lengths,
    norm_gain,
    in_weight,
    conv_weight,
    conv_bias,
    x_weight,
    dt_weight,
    dt_bias,
    a_log,
    skip_gain,
    out_weight,
):
    me = lax.axis_index("wsh")
    place = lax.axis_index("seq")
    seqs = lax.axis_size("wsh")
    seq_count = lax.axis_size("seq")
    tokens, width = hidden.shape[1:]
    inner = out_weight.shape[0]
    depth = in_weight.shape[0]
    states = a_log.shape[0]
    rank = dt_weight.shape[0]
    taps = conv_weight.shape[0]
    rows = seqs * tokens

    def slots(pieces):
        return [at_index(pieces, me ^ r, 0) for r in range(seqs)]

    at = jnp.stack([place, me]).astype(jnp.int32)

    quarter = depth // 4
    half = quarter // 2
    part = place % 4

    def columns_from(start, ready):
        def block(r, first, size):
            return lax.dynamic_slice(ready, (first, start + (me ^ r) * inner), (size, inner))

        sent = [block(r, part * quarter, quarter) for r in (2, 3)]
        far = [swap(v, r) for v, r in zip(sent, (2, 3))]
        return far, [block(0, 0, depth), swap(block(1, 0, depth), 1)], sent

    def over_seq(far):
        return [seq_xor(v, bit) for bit in (1, 2) for v in far]

    def ends(by):
        return [seq_xor(v[:half], 1) for v in by[2:]] + [seq_xor(v[half:], 2) for v in by[:2]]

    x_far, x_near, x_sent = columns_from(0, in_weight)

    note = jnp.concatenate([norm_gain.astype(F32), lengths.astype(F32), jnp.zeros((127,), F32)])
    notes = jnp.stack(spread_out(tied(note, x_sent)))
    gain = jnp.concatenate(slots(notes[:, : norm_gain.shape[0]]))
    slot_lengths = notes[:, norm_gain.shape[0]]
    count = jnp.sum(jnp.minimum(slot_lengths, seq_count * tokens))
    positions = place * tokens + lax.iota(jnp.int32, tokens)
    valid = (positions[None, :].astype(F32) < slot_lengths[:, None]).astype(F32)
    halo_positions = place * tokens - HALO + lax.iota(jnp.int32, HALO + tokens)
    halo_valid = (halo_positions[None, :].astype(F32) < slot_lengths[:, None]).astype(F32)

    rows_in = hidden[0].astype(F32)
    scale = lax.rsqrt(jnp.mean(rows_in * rows_in, axis=1, keepdims=True) + NORM_EPS)
    normed_own = (rows_in * scale * gain).astype(BF16)
    before = shifted(normed_own[tokens - HALO :], 1)
    normed_own = tied(jnp.concatenate([before, normed_own], axis=0), x_far)
    normed_one, normed_two = swap(normed_own, 1), swap(normed_own, 2)
    x_by = over_seq(x_far)
    x_ends = ends(x_by)
    normed_two, x_ends = lax.optimization_barrier((normed_two, x_ends))
    normed = [normed_own, normed_one, normed_two, swap(normed_two, 1)]
    x_columns = join(at, [*x_near, *x_far, *x_by, *x_ends], width)
    z_far, z_near, _ = columns_from(seqs * inner, tied(in_weight, normed_two))
    normed = jnp.stack(normed)
    normed_tokens = normed[:, HALO:].reshape(rows, width)

    x_both = product(normed.reshape(seqs * (HALO + tokens), width), x_columns, PLAIN)
    x_in = (x_both.reshape(seqs, HALO + tokens, inner) * halo_valid[:, :, None]).astype(BF16)
    padded = x_in[:, HALO - (taps - 1) :].astype(F32)
    conv_f = conv_weight.astype(F32)
    conv_out = conv_bias.astype(F32) + sum(
        conv_f[tap] * padded[:, tap : tap + tokens] for tap in range(taps)
    )
    conv_out = conv_out.reshape(rows, inner)
    act = silu_value(conv_out).astype(BF16)
    proj = sum_all(tied(product(x_weight, act, COLS_LAST), z_far)).astype(BF16)
    dt_low = proj[:rank]
    bc = proj[rank:].astype(F32)
    step = jax.nn.softplus(product(dt_low, dt_weight, ROWS_FIRST) + dt_bias.astype(F32))
    log_rate = a_log.astype(F32)
    rate = -jnp.exp(log_rate) * LOG2E
    skip = skip_gain.astype(F32)[None]

    z_by = over_seq(tied(z_far, step))
    last_far, total_far = p1(2, step, act, bc, rate, tokens)
    z_by, last_far, total_far = lax.optimization_barrier((z_by, last_far, total_far))
    z_ends = ends(z_by)
    carry_far = Carry(total_far, last_far, rate, False)
    last_near, total_near = p1(0, tied(step, last_far), act, bc, rate, tokens)
    z_ends, last_near, total_near = carry_far.held(z_ends, last_near, total_near)
    carry_far.second()
    carry_near = Carry(total_near, last_near, rate, False)
    z_columns = join(at, [*z_near, *z_far, *z_by, *z_ends], width)
    z_part = product(normed_tokens, z_columns, PLAIN)
    z_part = carry_near.held(carry_far.held(z_part))
    carry_near.second()
    carry_far = carry_far.result()
    mixed_far, gated_far, starts_far = p2(2, step, act, z_part, bc, rate, skip, carry_far, tokens)
    mixed_far, gated_far, starts_far = carry_near.held(mixed_far, gated_far, starts_far)
    carry_near = carry_near.result()

    def parts(gated):
        return product(gated, out_weight, PLAIN).reshape(2, tokens, width)

    far = parts(gated_far)
    far = swap((far[0] + swap(far[1].astype(BF16), 1).astype(F32)).astype(BF16), 2)
    mixed_near, gated_near, starts_near = p2(0, step, act, z_part, bc, rate, skip, carry_near, tokens)
    far, gated_near = lax.optimization_barrier((far, gated_near))
    near = parts(gated_near)
    near = near[0] + swap(near[1].astype(BF16), 1).astype(F32)
    full = rows_in + near + far.astype(F32)
    own_valid = valid[0][:, None]
    miss = full - teacher[0].astype(F32)
    g_full = cotangent[0].astype(F32) + 2.0 / (width * count) * own_valid * miss
    g_own = g_full.astype(BF16)
    loss_part = jnp.sum(own_valid * miss * miss)

    g_one, g_two = swap(g_own, 1), swap(g_own, 2)
    g_branch_near = jnp.concatenate([g_own, g_one], axis=0)

    def into_mixer(g_branch, mixed, first):
        z = z_part[first * tokens : (first + 2) * tokens]
        g_gated = product(g_branch, out_weight, COLS_LAST)
        return g_gated * silu_value(z), (g_gated * mixed * silu_slope(z)).astype(BF16)

    g_mixed_near, g_z_near = into_mixer(g_branch_near, mixed_near, 0)
    first_near = b1(0, step, g_mixed_near, bc, rate, tokens)
    g_two, first_near = lax.optimization_barrier((g_two, first_near))
    back_near = Carry(total_near, first_near, rate, True)
    g_branch_far = jnp.concatenate([g_two, swap(g_two, 1)], axis=0)
    gated = jnp.concatenate([gated_near, gated_far], axis=0)
    out_grad = product(gated, jnp.concatenate([g_branch_near, g_branch_far], axis=0), ROWS_FIRST).astype(BF16)
    by_steps = seq_count == 8
    g_mixed_far, g_z_far = into_mixer(g_branch_far, mixed_far, 2)
    g_mixed_far, g_z_far = back_near.held(g_mixed_far, g_z_far)
    back_near.second()
    first_far = b1(2, step, g_mixed_far, bc, rate, tokens)
    first_far = back_near.held(first_far)
    back_near = back_near.result()
    back_far = Carry(total_far, first_far, rate, True)
    g_z = jnp.concatenate([g_z_near, g_z_far], axis=0)

    def in_shares(g, normed):
        return product(normed, g, ROWS_FIRST).astype(BF16).reshape(seqs, seq_count, depth // seq_count, g.shape[1])

    def way(v, d):
        wide = v.shape[-1] // 2
        return v[..., d * wide : (d + 1) * wide]

    def in_chunk(shares):
        return lambda d, q: at_index(way(shares, d), q, 1).reshape(width // seq_count, inner // 2)

    def in_between(own):
        return [crossed_blocks(v.reshape(seqs, -1, inner // 2)).reshape(v.shape) for v in own]

    out_own = reduced(out_grad)
    pair_near = (step, act, g_mixed_near, bc, rate, skip, starts_near, back_near, tokens)
    zero = b2(0, 1, None, *pair_near)
    zero = back_far.held(*zero)
    back_far.second()
    g_z = tied(g_z, zero)
    z_shares = jnp.swapaxes(in_shares(g_z, normed_tokens), 0, 1).reshape(width, inner)
    one = b2(1, 1, zero[:2], *pair_near)
    one = back_far.held(*one)
    back_far = back_far.result()
    z_shares, back_far = lax.optimization_barrier((z_shares, back_far))
    pair_far = (step, act, g_mixed_far, bc, rate, skip, starts_far, back_far, tokens)
    out_own, z_shares, *one = lax.optimization_barrier((out_own, z_shares, *one))
    z_own = reduced(z_shares)
    early = [Ring(None, None, [way(out_own, d) for d in range(2)])] if by_steps else []
    two = b2(2, 1, one[:2], *pair_far)
    two = advance(early, *two)
    three = b2(3, 1, two[:2], *pair_far)
    three = advance(early, *three)
    far = [*three[:2], *[jnp.concatenate([v, w]) for v, w in zip(two[2:], three[2:])]]
    near = [jnp.concatenate([v, w]) for v, w in zip(zero[2:], one[2:])]
    g_pre, g_act_part = far[:2]
    g_b, g_c = [jnp.concatenate([near[i], far[2 + i]]).reshape(rows, states).T for i in (0, 1)]
    rate_sum, sums = [jnp.sum(near[i] + far[2 + i], axis=0) for i in (2, 3)]
    dt_bias_grad, skip_grad = jnp.sum(sums, axis=1)
    g_dt_low = product(dt_weight, g_pre, COLS_LAST)
    g_proj = sum_all(
        jnp.concatenate([g_dt_low, g_b, g_c], axis=0)
    ).astype(BF16)
    g_proj = advance(early, g_proj)
    g_act = g_act_part + product(g_proj, x_weight, ROWS_FIRST)
    g_conv = (g_act * silu_slope(conv_out)).reshape(seqs, tokens, inner)
    g_padded = jnp.pad(g_conv, ((0, 0), (HALO, taps - 1), (0, 0)))
    g_x = sum(
        conv_f[tap] * g_padded[:, taps - 1 - tap : taps - 1 - tap + HALO + tokens] for tap in range(taps)
    )
    g_x = (g_x * halo_valid[:, :, None]).astype(BF16)
    conv_grad = [jnp.sum(g_conv * padded[:, tap : tap + tokens], axis=(0, 1)) for tap in range(taps)]
    small = [
        product(g_proj, act, PLAIN),
        product(dt_low, g_pre, PLAIN),
        rate_sum * (rate * LN2),
        jnp.stack(conv_grad),
        jnp.sum(g_conv, axis=(0, 1))[None],
        dt_bias_grad[None],
        skip_grad[None],
    ]
    cut = [0]
    for piece in small:
        cut.append(cut[-1] + piece.shape[0])
    lines = 16 * seq_count
    small.append(jnp.zeros((-cut[-1] % lines, inner), F32))
    small = jnp.concatenate(small, axis=0)
    normed_all = normed.reshape(seqs * (HALO + tokens), width)
    g_x_all = g_x.reshape(seqs * (HALO + tokens), inner)
    if by_steps:
        x_shares = in_shares(g_x_all, normed_all)
        small_shares = small.astype(BF16).reshape(seq_count, -1, inner)
        z_own, x_shares, small_shares, g_x = advance(early, z_own, x_shares, small_shares, g_x)
        large = width // seq_count
        chunk_of = in_chunk(x_shares)

        def x_chunk(d, q):
            return jnp.concatenate([chunk_of(d, q), at_index(way(small_shares, d), q, 0)], axis=0)

        def x_between(own):
            return [jnp.concatenate([x, v[large:]], axis=0) for x, v in zip(in_between([v[:large] for v in own]), own)]

        x_ring = Ring(x_chunk, x_between)
        out_ring = early[0]
        z_row = crossed_blocks(z_own.reshape(seqs, -1, inner)).reshape(-1, inner)
        rings = [x_ring, out_ring]
        z_row, g_x = advance(rings, z_row, g_x)
        z_ring = Ring(None, None, [way(z_row, d) for d in range(2)])
        rings.append(z_ring)
    after = shifted(g_x[:, HALO - (taps - 1) : HALO], -1)
    g_z = tied(g_z, g_x)

    def to_normed(g, columns, slot):
        return product(g[slot * tokens : (slot + 1) * tokens], columns, COLS_LAST)

    def advanced(*v):
        if by_steps:
            return advance([ring for ring in rings if not ring.done()], *v)
        return v[0] if len(v) == 1 else v

    normed_1, normed_3 = advanced(to_normed(g_z, z_columns, 1), to_normed(g_z, z_columns, 3))
    normed_2, after = advanced(to_normed(g_z, z_columns, 2), after)
    fixed = jnp.pad(after, ((0, 0), (tokens - (taps - 1), 0), (0, 0)))
    g_x = advanced((g_x[:, HALO:] + fixed).reshape(rows, inner))
    normed_1 += to_normed(g_x, x_columns, 1)
    normed_3 += to_normed(g_x, x_columns, 3)
    ready = ()
    if by_steps:
        where = jnp.stack([me] + ring_order()).astype(jnp.int32)
        out_is = partial(settle, where, out_ring.result(), out_weight.shape, 1, width)
        ready = (out_is(part=0)[0],)
    normed_1, normed_3, *ready = advanced(normed_1.astype(BF16), normed_3.astype(BF16), *ready)
    got1, got3 = swap((normed_1, normed_3), 1)
    if by_steps:
        ready = (out_is(part=1, filled=ready[0])[0],)
    got1, got3, normed_2, *ready = advanced(got1, got3, normed_2 + to_normed(g_x, x_columns, 2), *ready)
    normed_0 = advanced(to_normed(g_z, z_columns, 0))
    other = swap(tied((normed_2 + got3.astype(F32)).astype(BF16), normed_0), 2)
    normed_0 = advanced(normed_0 + to_normed(g_x, x_columns, 0) + got1.astype(F32))
    if by_steps:
        (out_owned,) = ready
        z_is = partial(settle, where, z_ring.result(), in_weight.shape, seqs, inner, half=1)
        assert out_ring.done() and z_ring.done()
        in_owned = advanced(z_is(part=0)[0])
        other, in_owned = advanced(other, z_is(part=1, filled=in_owned)[0])
    g_normed = normed_0 + other.astype(F32)
    gain_part = jnp.sum(g_normed * rows_in * scale, axis=0)
    tail = jnp.concatenate([gain_part, jnp.full((128,), loss_part)])
    if by_steps:
        for bit in (1, 2, 4):
            tail = advanced(tail + seq_xor(tail, bit))
    else:
        tail = lax.psum(tail, "seq")
    gain_share = slots(tail[:width].reshape(seqs, -1))
    gain_grad = gain_share[0] + sum(swap(gain_share[r], r) for r in range(1, seqs))
    loss_sum = tail[width:] + swap(tail[width:], 1)
    loss = (loss_sum + swap(loss_sum, 2))[0] / (width * count)
    if by_steps:
        gain_grad, loss, in_owned = advanced(gain_grad, loss, in_owned)
        while not x_ring.done():
            in_owned = advanced(in_owned)
        in_owned, small = settle(
            where, x_ring.result(), in_weight.shape, seqs, inner, filled=in_owned, extra=small.shape[0]
        )
    if not by_steps:
        x_shares = jnp.swapaxes(in_shares(g_x_all, normed_all), 0, 1)
        x_row = crossed_blocks(reduced(x_shares.reshape(width, inner)).reshape(seqs, -1, inner))
        x_owned = lax.all_gather(jnp.concatenate(slots(x_row), axis=1), "seq", axis=0, tiled=True)
        small = lax.psum(small, "seq")
        out_owned = lax.all_gather(out_own, "seq", axis=0, tiled=True)
        out_owned = spread_rows([out_owned], out_weight.shape)
        in_owned = spread_rows([x_owned], in_weight.shape)
        z_row = crossed_blocks(z_own.reshape(seqs, -1, inner))
        z_owned = lax.all_gather(jnp.concatenate(slots(z_row), axis=1), "seq", axis=0, tiled=True)
        in_owned = spread_rows([z_owned], in_weight.shape, 1, in_owned)
    x_grad, dt_grad, log_rate_grad, conv_grad, conv_bias_grad, dt_bias_grad, skip_grad = cut_rows(small, cut)
    weighted = g_normed * gain
    g_rows = (
        g_full
        + scale * weighted
        - rows_in * scale * scale * scale * jnp.mean(weighted * rows_in, axis=1, keepdims=True)
    )
    return (
        full[None].astype(BF16),
        loss,
        g_rows[None].astype(BF16),
        gain_grad,
        in_owned,
        conv_grad,
        conv_bias_grad[0],
        x_grad,
        dt_grad,
        dt_bias_grad[0],
        log_rate_grad,
        skip_grad[0],
        out_owned,
    )


def solution(mesh):
    rows = P("wsh", "seq", None)
    first, second = P("wsh", None), P(None, "wsh")
    one = P("wsh")
    return jax.shard_map(
        local,
        mesh=mesh,
        in_specs=(
            rows, rows, rows, one, one, first, second, one, second, second, one, second, one, first,
        ),
        out_specs=(
            rows, P(), rows, one, first, second, one, second, second, one, second, one, first,
        ),
        check_vma=False,
    )
```

```python
from functools import partial

import jax
import jax.numpy as jnp
from jax import lax
from jax.experimental import pallas as pl
from jax.experimental.pallas import tpu as pltpu
from jax.sharding import PartitionSpec as P

F32 = jnp.float32
BF16 = jnp.bfloat16
NORM_EPS = 1e-05
LOG2E = 1.4426950408889634
LN2 = 0.6931471805599453
GROUP = 8
CHUNK = 32
HALO = 16
VMEM_LIMIT = 56 * 1024 * 1024
ROWS_FIRST = (((0,), (0,)), ((), ()))
COLS_LAST = (((1,), (1,)), ((), ()))
PLAIN = (((1,), (0,)), ((), ()))


def product(left, right, dims):
    return lax.dot_general(left, right, dims, preferred_element_type=F32)


def silu_value(v):
    return v * jax.nn.sigmoid(v)


def silu_slope(v):
    sigma = jax.nn.sigmoid(v)
    return sigma * (1.0 + v * (1.0 - sigma))


def kernel_params():
    return pltpu.CompilerParams(vmem_limit_bytes=VMEM_LIMIT)


def cost(microseconds):
    return pl.CostEstimate(flops=int(microseconds * 1e9), bytes_accessed=0, transcendentals=0)


def widen(bc_ref, row, size, rep_ref):
    ones = jnp.ones((128, 128), BF16)
    lane = lax.broadcasted_iota(jnp.int32, (size, 128), 1)
    part = 32

    def block(i, _):
        t0 = pl.multiple_of(i * 128, 128)
        x = bc_ref[row : row + size, pl.ds(t0, 128)]
        for j in range(0, 128, part):
            picked = jnp.concatenate([jnp.where(lane == k, x, 0.0) for k in range(j, j + part)], axis=0)
            wide = jnp.dot(picked.astype(BF16), ones, preferred_element_type=F32)
            rep_ref[pl.ds(t0 + j, part)] = wide.reshape(part, size, 128)
        return 0

    lax.fori_loop(0, bc_ref.shape[1] // 128, block, 0)


def tiled(x, width):
    return jnp.concatenate([x]*(width//128), axis=1)

def put_fold(fold_ref,k,v):
    for i in range(v.shape[1]//128):
        fold_ref[i,8*k:8*k+8,:]=v[:,128*i:128*i+128]

def get_fold(fold_ref):
    def tree(x):
        while len(x)>1: x=[a+b for a,b in zip(x[::2],x[1::2])]
        return x[0]
    return jnp.concatenate([tree([fold_ref[i,pl.ds(r,GROUP,stride=8),:] for r in range(8)]) for i in range(fold_ref.shape[0])],axis=1)

def p1_kernel(step_ref, act_ref, bc_ref, rate_ref, last_ref, total_ref, dx_ref, brep_ref, *, eb, n):
    widen(bc_ref,0,n,brep_ref)
    step=step_ref[...]
    dx_ref[...]=step*act_ref[...].astype(F32)
    total_ref[0]=jnp.sum(step,axis=0,keepdims=True)
    tokens,width=step_ref.shape
    for e in range(0,width,eb):
        sl=slice(e,e+eb)
        rate=rate_ref[:,sl]
        def group(g,h):
            base=pl.multiple_of(g*GROUP,GROUP)
            s8=step_ref[pl.ds(base,GROUP),sl]
            x8=dx_ref[pl.ds(base,GROUP),sl]
            for k in range(GROUP):
                d=jnp.exp2(rate*s8[k:k+1])
                h=d*h+tiled(brep_ref[base+k],eb)*x8[k:k+1]
            return h
        last_ref[0,:,sl]=lax.fori_loop(0,tokens//GROUP,group,jnp.zeros((n,eb),F32))

def p1(first, step, act, bc, rate, tokens, eb=1024):
    width = step.shape[1]
    n = rate.shape[0]
    blk = pl.BlockSpec((tokens, width), lambda s: (first + s, 0))
    return pl.pallas_call(
        partial(p1_kernel, eb=eb, n=n),
        grid=(2,),
        in_specs=[
            blk,
            blk,
            pl.BlockSpec((bc.shape[0], tokens), lambda s: (0, first + s)),
            pl.BlockSpec((n, width), lambda s: (0, 0)),
        ],
        out_specs=[
            pl.BlockSpec((1, n, width), lambda s: (s, 0, 0)),
            pl.BlockSpec((1, 1, width), lambda s: (s, 0, 0)),
        ],
        out_shape=[jax.ShapeDtypeStruct((2, n, width), F32), jax.ShapeDtypeStruct((2, 1, width), F32)],
        scratch_shapes=[pltpu.VMEM((tokens, width), F32), pltpu.VMEM((tokens, n, 128), F32)],
        cost_estimate=cost(9),
        compiler_params=kernel_params(),
    )(step, act, bc, rate)


def p2_kernel(step_ref, act_ref, z_ref, bc_ref, rate_ref, skip_ref, carry_ref, mixed_ref, gated_ref, starts_ref, dx_ref, fold_ref, brep_ref, crep_ref, *, eb, n):
    widen(bc_ref,0,n,brep_ref)
    widen(bc_ref,n,n,crep_ref)
    dx_ref[...]=step_ref[...]*act_ref[...].astype(F32)
    tokens,width=step_ref.shape
    for e in range(0,width,eb):
        sl=slice(e,e+eb)
        rate=rate_ref[:,sl]
        def chunk(c,h):
            starts_ref[0,c,:,sl]=h
            def group(j,h):
                g=c*(CHUNK//GROUP)+j
                base=pl.multiple_of(g*GROUP,GROUP)
                s8=step_ref[pl.ds(base,GROUP),sl]
                x8=dx_ref[pl.ds(base,GROUP),sl]
                for k in range(GROUP):
                    d=jnp.exp2(rate*s8[k:k+1])
                    h=d*h+tiled(brep_ref[base+k],eb)*x8[k:k+1]
                    p=tiled(crep_ref[base+k],eb)*h
                    put_fold(fold_ref,k,sum(p[8*i:8*i+8] for i in range(n//8)))
                mixed_ref[pl.ds(base,GROUP),sl]=get_fold(fold_ref)
                return h
            return lax.fori_loop(0,CHUNK//GROUP,group,h)
        lax.fori_loop(0,tokens//CHUNK,chunk,carry_ref[0,:,sl])
    def gate(i,_):
        rows=pl.ds(pl.multiple_of(i*16,16),16)
        m=mixed_ref[rows,:]+skip_ref[...]*act_ref[rows,:].astype(F32)
        mixed_ref[rows,:]=m
        z=z_ref[rows,:]
        gated_ref[rows,:]=(m*(z*jax.nn.sigmoid(z))).astype(BF16)
        return 0
    lax.fori_loop(0,tokens//16,gate,0)

def p2(first, step, act, z, bc, rate, skip, carry, tokens, eb=1024):
    width = step.shape[1]
    n = rate.shape[0]
    nch = tokens // CHUNK
    blk = pl.BlockSpec((tokens, width), lambda s: (first + s, 0))
    out = pl.BlockSpec((tokens, width), lambda s: (s, 0))
    rep = pltpu.VMEM((tokens, n, 128), F32)
    return pl.pallas_call(
        partial(p2_kernel, eb=eb, n=n),
        grid=(2,),
        in_specs=[
            blk,
            blk,
            blk,
            pl.BlockSpec((bc.shape[0], tokens), lambda s: (0, first + s)),
            pl.BlockSpec((n, width), lambda s: (0, 0)),
            pl.BlockSpec((1, width), lambda s: (0, 0)),
            pl.BlockSpec((1, n, width), lambda s: (s, 0, 0)),
        ],
        out_specs=[out, out, pl.BlockSpec((1, nch, n, width), lambda s: (s, 0, 0, 0))],
        out_shape=[
            jax.ShapeDtypeStruct((2 * tokens, width), F32),
            jax.ShapeDtypeStruct((2 * tokens, width), BF16),
            jax.ShapeDtypeStruct((2, nch, n, width), F32),
        ],
        scratch_shapes=[pltpu.VMEM((tokens, width), F32), pltpu.VMEM((eb // 128, 64, 128), F32), rep, rep],
        cost_estimate=cost(16),
        compiler_params=kernel_params(),
    )(step, act, z, bc, rate, skip, carry)


def b1_kernel(step_ref, dy_ref, bc_ref, rate_ref, first_ref, crep_ref, *, eb, n):
    widen(bc_ref,n,n,crep_ref)
    tokens,width=step_ref.shape
    for e in range(0,width,eb):
        sl=slice(e,e+eb)
        rate=rate_ref[:,sl]
        def group(j,h):
            g=tokens//GROUP-1-j
            base=pl.multiple_of(g*GROUP,GROUP)
            s8=step_ref[pl.ds(base,GROUP),sl]
            y8=dy_ref[pl.ds(base,GROUP),sl]
            for k in reversed(range(GROUP)):
                h=jnp.exp2(rate*s8[k:k+1])*(h+tiled(crep_ref[base+k],eb)*y8[k:k+1])
            return h
        first_ref[0,:,sl]=lax.fori_loop(0,tokens//GROUP,group,jnp.zeros((n,eb),F32))

def b1(first, step, dy, bc, rate, tokens, eb=1024):
    width = step.shape[1]
    n = rate.shape[0]
    return pl.pallas_call(
        partial(b1_kernel, eb=eb, n=n),
        grid=(2,),
        in_specs=[
            pl.BlockSpec((tokens, width), lambda s: (first + s, 0)),
            pl.BlockSpec((tokens, width), lambda s: (s, 0)),
            pl.BlockSpec((bc.shape[0], tokens), lambda s: (0, first + s)),
            pl.BlockSpec((n, width), lambda s: (0, 0)),
        ],
        out_specs=pl.BlockSpec((1, n, width), lambda s: (s, 0, 0)),
        out_shape=jax.ShapeDtypeStruct((2, n, width), F32),
        scratch_shapes=[pltpu.VMEM((tokens, n, 128), F32)],
        cost_estimate=cost(9),
        compiler_params=kernel_params(),
    )(step, dy, bc, rate)


def one_less_exp(s):
    return jnp.where(s<0.01, s*(1.0-s*(0.5-s*(1.0/6.0))), 1.0-jnp.exp(-s))

def b2_kernel(step_ref, act_ref, dy_ref, bc_ref, rate_ref, skip_ref, starts_ref, carry_ref, *refs, eb, n):
    (gpre_ref, gact_ref, gb_ref, gc_ref, alog_ref, dtb_ref, dx_ref, prev_ref, dec_ref, folda_ref, folds_ref,
     pb_ref, pc_ref, g_ref, brep_ref, crep_ref) = refs[-16:]
    widen(bc_ref,0,n,brep_ref)
    widen(bc_ref,n,n,crep_ref)
    tokens,width=step_ref.shape
    nch=tokens//CHUNK; per=CHUNK//GROUP
    dx_ref[...]=step_ref[...]*act_ref[...].astype(F32)
    g_ref[...]=carry_ref[0]
    alog_ref[...]=jnp.zeros_like(alog_ref)
    ones=jnp.ones((8,128),F32)
    def chunk(cc,_):
        c=nch-1-cc
        for e in range(0,width,eb):
            sl=slice(e,e+eb)
            rate=rate_ref[:,sl]
            def redo(j,h):
                g=c*per+j
                base=pl.multiple_of(g*GROUP,GROUP)
                s8=step_ref[pl.ds(base,GROUP),sl]
                x8=dx_ref[pl.ds(base,GROUP),sl]
                for k in range(GROUP):
                    d=jnp.exp2(rate*s8[k:k+1])
                    prev_ref[j*GROUP+k]=h
                    dec_ref[j*GROUP+k]=d
                    h=d*h+tiled(brep_ref[base+k],eb)*x8[k:k+1]
                return h
            last=lax.fori_loop(0,per,redo,starts_ref[0,c,:,sl])
            def back(jj,carry):
                h,alog,after=carry
                j=per-1-jj
                g=c*per+j
                base=pl.multiple_of(g*GROUP,GROUP)
                s8=step_ref[pl.ds(base,GROUP),sl]
                x8=dx_ref[pl.ds(base,GROUP),sl]
                y8=dy_ref[pl.ds(base,GROUP),sl]
                for k in reversed(range(GROUP)):
                    s=s8[k:k+1]
                    g_state=tiled(crep_ref[base+k],eb)*y8[k:k+1]+h
                    prev=prev_ref[j*GROUP+k]
                    pc=after*y8[k:k+1]
                    pb=g_state*x8[k:k+1]
                    al=g_state*tiled(brep_ref[base+k],eb)
                    h=g_state*dec_ref[j*GROUP+k]
                    q=h*prev
                    alog=alog+q*s
                    qs=q*rate
                    pcs=sum(pc[:,i:i+128] for i in range(0,eb,128))
                    pbs=sum(pb[:,i:i+128] for i in range(0,eb,128))
                    rows=pl.ds(pl.multiple_of((j*GROUP+k)*n,n),n)
                    if e==0:
                        pc_ref[rows,:]=pcs; pb_ref[rows,:]=pbs
                    else:
                        pc_ref[rows,:]+=pcs; pb_ref[rows,:]+=pbs
                    put_fold(folda_ref,k,sum(al[8*i:8*i+8] for i in range(n//8)))
                    put_fold(folds_ref,k,sum(qs[8*i:8*i+8] for i in range(n//8)))
                    after=prev
                gact_ref[pl.ds(base,GROUP),sl]=get_fold(folda_ref)
                dx_ref[pl.ds(base,GROUP),sl]=get_fold(folds_ref)
                return h,alog,after
            h,alog,_u=lax.fori_loop(0,per,back,(g_ref[:,sl],jnp.zeros((n,eb),F32),last))
            g_ref[:,sl]=h
            alog_ref[0,:,sl]+=alog
        for j in range(per):
            part=pb_ref[j*128:(j+1)*128,:]
            gb_ref[0,pl.ds(c*per+j,1),:]=lax.dot_general(ones,part,(((1,),(1,)),((),())),precision=lax.Precision.HIGHEST,preferred_element_type=F32)[0:1]
            part=pc_ref[j*128:(j+1)*128,:]
            gc_ref[0,pl.ds(c*per+j,1),:]=lax.dot_general(ones,part,(((1,),(1,)),((),())),precision=lax.Precision.HIGHEST,preferred_element_type=F32)[0:1]
        return 0
    lax.fori_loop(0,nch,chunk,0)
    def finish(i,acc):
        rows=pl.ds(pl.multiple_of(i*16,16),16)
        s=step_ref[rows,:]; along=gact_ref[rows,:]
        a=act_ref[rows,:].astype(F32)
        garg=(dx_ref[rows,:]*LN2+a*along)*one_less_exp(s)
        gpre_ref[rows,:]=garg.astype(BF16)
        dy=dy_ref[rows,:]
        gact_ref[rows,:]=dy*skip_ref[...]+s*along
        return acc[0]+jnp.sum(garg.reshape(2,8,width),axis=0), acc[1]+jnp.sum((dy*a).reshape(2,8,width),axis=0)
    zero=jnp.zeros((8,width),F32)
    acc=lax.fori_loop(0,tokens//16,finish,(zero,zero))
    dtb_ref[0,0]=acc[0]
    dtb_ref[0,1]=acc[1]

def b2(first, count, filled, step, act, dy, bc, rate, skip, starts, carry, tokens, eb=512):
    base = first % 2
    rows, width = step.shape
    n = rate.shape[0]
    nch = tokens // CHUNK
    blk = pl.BlockSpec((tokens, width), lambda i: (first + i, 0))
    full = lambda shape: pl.BlockSpec(shape, lambda i: (0,) * len(shape))
    own = lambda shape: pl.BlockSpec((1, *shape[1:]), lambda i: (i,) + (0,) * (len(shape) - 1))
    red = (count, tokens // GROUP, 128)
    rep = pltpu.VMEM((tokens, n, 128), F32)
    held = pltpu.VMEM((CHUNK, n, eb), F32)
    fold = pltpu.VMEM((eb // 128, 64, 128), F32)
    part = pltpu.VMEM((CHUNK * n, 128), F32)
    extra = () if filled is None else tuple(filled)
    return pl.pallas_call(
        partial(b2_kernel, eb=eb, n=n),
        grid=(count,),
        in_specs=[
            blk,
            blk,
            pl.BlockSpec((tokens, width), lambda i: (base + i, 0)),
            pl.BlockSpec((bc.shape[0], tokens), lambda i: (0, first + i)),
            full((n, width)),
            full((1, width)),
            pl.BlockSpec((1, nch, n, width), lambda i: (base + i, 0, 0, 0)),
            pl.BlockSpec((1, n, width), lambda i: (base + i, 0, 0)),
        ]
        + [pl.BlockSpec(memory_space=pl.ANY)] * len(extra),
        out_specs=[blk, blk, own(red), own(red), own((count, n, width)), own((count, 2, 8, width))],
        out_shape=[
            jax.ShapeDtypeStruct((rows, width), BF16),
            jax.ShapeDtypeStruct((rows, width), F32),
            jax.ShapeDtypeStruct(red, F32),
            jax.ShapeDtypeStruct(red, F32),
            jax.ShapeDtypeStruct((count, n, width), F32),
            jax.ShapeDtypeStruct((count, 2, 8, width), F32),
        ],
        scratch_shapes=[
            pltpu.VMEM((tokens, width), F32),
            held,
            held,
            fold,
            fold,
            part,
            part,
            pltpu.VMEM((n, width), F32),
            rep,
            rep,
        ],
        input_output_aliases={8: 0, 9: 1} if extra else {},
        cost_estimate=cost(25 * count),
        compiler_params=kernel_params(),
    )(step, act, dy, bc, rate, skip, starts, carry, *extra)


def settle_kernel(at_ref, *refs, steps, base, blocks, cols, extra):
    out_ref = refs[-2] if extra else refs[-1]
    rows = out_ref.shape[0]
    i = base + pl.program_id(0)
    for d in range(2):
        for k in range(steps):
            ref = refs[d * steps + k]
            wide = ref.shape[1]

            @pl.when(at_ref[1 + d * steps + i] == k)
            def _():
                for r in range(blocks):
                    start = d * wide
                    if blocks > 1:
                        start = pl.multiple_of((at_ref[0] ^ r) * cols + start, 128)
                    out_ref[:, pl.ds(start, wide)] = ref[r * rows : (r + 1) * rows, :].astype(F32)
                if extra:
                    refs[-1][:, d * wide : (d + 1) * wide] = ref[blocks * rows :, :].astype(F32)


def settle(at, both, shape, blocks, cols, half=0, filled=None, extra=0, part=None):
    steps = len(both[0])
    rows, wide = both[0][0].shape
    piece = (rows - extra // steps) // blocks
    span = blocks * cols if blocks > 1 else 2 * wide
    given = [] if filled is None else [filled]
    count, base = (steps, 0) if part is None else (steps // 2, part * steps // 2)
    out_specs = [pl.BlockSpec((piece, span), lambda i, at_ref: (base + i, half))]
    out_shape = [jax.ShapeDtypeStruct(shape, F32)]
    if extra:
        out_specs.append(pl.BlockSpec((extra // steps, 2 * wide), lambda i, at_ref: (base + i, 0)))
        out_shape.append(jax.ShapeDtypeStruct((extra, 2 * wide), F32))
    whole = pl.BlockSpec((rows, wide), lambda i, at_ref: (0, 0))
    return pl.pallas_call(
        partial(settle_kernel, steps=steps, base=base, blocks=blocks, cols=cols, extra=extra),
        grid_spec=pltpu.PrefetchScalarGridSpec(
            num_scalar_prefetch=1,
            grid=(count,),
            in_specs=[whole] * (2 * steps) + [pl.BlockSpec(memory_space=pl.ANY)] * len(given),
            out_specs=out_specs,
        ),
        out_shape=out_shape,
        input_output_aliases={1 + 2 * steps: 0} if given else {},
        cost_estimate=cost(7 if part is None else 4),
        compiler_params=kernel_params(),
    )(at, *both[0], *both[1], *given)


def settle_some_kernel(at_ref, *refs, count, blocks, cols):
    out_ref, small_ref = refs[-2:]
    rows = out_ref.shape[0]
    for j in range(count):

        @pl.when(pl.program_id(0) == j)
        def _():
            for d in range(2):
                ref = refs[2 * j + d]
                wide = ref.shape[1]
                for r in range(blocks):
                    start = pl.multiple_of((at_ref[0] ^ r) * cols + d * wide, 128)
                    out_ref[:, pl.ds(start, wide)] = ref[r * rows : (r + 1) * rows, :].astype(F32)
                small_ref[:, d * wide : (d + 1) * wide] = ref[blocks * rows :, :].astype(F32)


def settle_some(me, devices, both, turns, shape, blocks, cols, extra, filled):
    steps = len(RING)
    pairs = [(both[0][t], both[1][(steps - t) % steps]) for t in turns]
    rows, wide = pairs[0][0].shape
    piece = (rows - extra // steps) // blocks
    whole = pl.BlockSpec((rows, wide), lambda i, at_ref: (0, 0))
    return pl.pallas_call(
        partial(settle_some_kernel, count=len(turns), blocks=blocks, cols=cols),
        grid_spec=pltpu.PrefetchScalarGridSpec(
            num_scalar_prefetch=1,
            grid=(len(turns),),
            in_specs=[whole] * (2 * len(turns)) + [pl.BlockSpec(memory_space=pl.ANY)] * len(filled),
            out_specs=[
                pl.BlockSpec((piece, blocks * cols), lambda i, at_ref: (at_ref[1 + i], 0)),
                pl.BlockSpec((extra // steps, 2 * wide), lambda i, at_ref: (at_ref[1 + i], 0)),
            ],
        ),
        out_shape=[jax.ShapeDtypeStruct(shape, F32), jax.ShapeDtypeStruct((extra, 2 * wide), F32)],
        input_output_aliases={1 + 2 * len(turns) + j: j for j in range(len(filled))},
        cost_estimate=cost(len(turns)),
        compiler_params=kernel_params(),
    )(jnp.stack([me] + devices).astype(jnp.int32), *[v for pair in pairs for v in pair], *filled)


def cut_rows_kernel(v_ref, *out_refs, cut):
    for ref, first in zip(out_refs, cut):
        ref[...] = v_ref[first : first + ref.shape[0], :]


def cut_rows(v, cut):
    whole = pl.BlockSpec(memory_space=pltpu.VMEM)
    sizes = [b - a for a, b in zip(cut, cut[1:])]
    return pl.pallas_call(
        partial(cut_rows_kernel, cut=cut),
        in_specs=[whole],
        out_specs=[whole] * len(sizes),
        out_shape=[jax.ShapeDtypeStruct((size, v.shape[1]), F32) for size in sizes],
        cost_estimate=cost(2),
        compiler_params=kernel_params(),
    )(v)


def spread_rows_kernel(*refs, count):
    out_ref = refs[-1]
    wide = refs[0].shape[1]
    for h in range(count):
        out_ref[:, h * wide : (h + 1) * wide] = refs[h][...].astype(F32)


def spread_rows(parts, shape, half=0, filled=None, part=None):
    rows, wide = parts[0].shape
    given = [] if filled is None else [filled]
    count, base = (8, 0) if part is None else (4, 4 * part)
    return pl.pallas_call(
        partial(spread_rows_kernel, count=len(parts)),
        grid=(count,),
        in_specs=[pl.BlockSpec((rows // 8, wide), lambda i: (base + i, 0))] * len(parts)
        + [pl.BlockSpec(memory_space=pl.ANY)] * len(given),
        out_specs=pl.BlockSpec((rows // 8, wide * len(parts)), lambda i: (base + i, half)),
        out_shape=jax.ShapeDtypeStruct(shape, F32),
        input_output_aliases={len(parts): 0} if given else {},
        cost_estimate=cost(4),
        compiler_params=kernel_params(),
    )(*parts, *given)


def join_kernel(at_ref, *refs):
    part, me = at_ref[0] % 4, at_ref[1]
    near_ref, next_ref, *far_refs, out_ref = refs
    depth = near_ref.shape[0]
    quarter = depth // 4
    half = quarter // 2

    def put(row, ref):
        out_ref[pl.ds(pl.multiple_of(row, half), ref.shape[0]), :] = ref[...]

    put(me * depth, near_ref)
    put((me ^ 1) * depth, next_ref)
    for k in range(2):
        start = (me ^ (2 + k)) * depth
        own, one, two, end, tail = far_refs[k::2]
        put(start + part * quarter, own)
        put(start + (part ^ 1) * quarter, one)
        put(start + (part ^ 2) * quarter, two)
        put(start + (part ^ 3) * quarter, end)
        put(start + (part ^ 3) * quarter + half, tail)


def join(at, pieces, rows):
    wide = pieces[0].shape[1]
    return pl.pallas_call(
        join_kernel,
        in_specs=[pl.BlockSpec(memory_space=pltpu.SMEM)] + [pl.BlockSpec(memory_space=pltpu.VMEM)] * len(pieces),
        out_specs=pl.BlockSpec(memory_space=pltpu.VMEM),
        out_shape=jax.ShapeDtypeStruct((rows, wide), BF16),
        cost_estimate=cost(4),
        compiler_params=kernel_params(),
    )(at, *pieces)


def swap(v, bit):
    return jax.tree.map(
        lambda a: lax.ppermute(a, "wsh", [(i, i ^ bit) for i in range(lax.axis_size("wsh"))]), v
    )


def shifted(v, distance):
    count = lax.axis_size("seq")
    route = [(i - distance, i) for i in range(count) if 0 <= i - distance < count]
    return jax.tree.map(lambda a: lax.ppermute(a, "seq", route), v)


def spread_out(v):
    one = swap(v, 1)
    two = swap(v, 2)
    return [v, one, two, swap(two, 1)]


def sum_to_owner(parts, own_cast=BF16):
    got1, got3 = swap((parts[1].astype(own_cast), parts[3].astype(own_cast)), 1)
    mine = parts[0] + got1.astype(F32)
    other = (parts[2] + got3.astype(F32)).astype(own_cast)
    return mine + swap(other, 2).astype(F32)


def crossed(v, bit):
    got = jnp.split(swap(v, bit), lax.axis_size("wsh"), axis=1)
    return jnp.concatenate([got[r ^ bit] for r in range(len(got))], axis=1)


def sum_all(v):
    v = v + crossed(v, 1)
    return v + crossed(v.astype(BF16), 2).astype(F32)


def hi_lo(v):
    hi = v.astype(BF16)
    return [hi, (v - hi.astype(F32)).astype(BF16)]


def carried_far(total, state, rate, reverse):
    count = lax.axis_size("seq")
    sign = -1 if reverse else 1
    total, state = shifted((total, state), sign)
    hop = 1
    while hop < count:
        got_total, got_state = shifted((total, state), sign * hop)
        state = state + jnp.exp2(rate[None] * total) * got_state
        total = total + got_total
        hop *= 2
    return state


class Carry:
    def __init__(self, total, state, rate, reverse):
        self.total, self.rate, self.reverse = total, rate, reverse
        self.near = lax.axis_size("seq") == 8
        if self.near:
            self.state = state
            self.moved = [seq_xor(self.packed(total, state), 1)]
        else:
            self.moved = [carried_far(total, state, rate, reverse)]

    def held(self, *others):
        count = len(self.moved)
        got = lax.optimization_barrier((*self.moved, *others))
        self.moved = list(got[:count])
        return got[count] if len(others) == 1 else got[count:]

    def packed(self, t, s):
        return jnp.concatenate([s.astype(BF16)] + hi_lo(t), axis=1)

    def opened(self, v):
        v = v.astype(F32)
        n = self.rate.shape[0]
        return v[:, n : n + 1] + v[:, n + 1 : n + 2], v[:, :n]

    def fall(self, t):
        return jnp.exp2(self.rate[None] * t)

    def second(self):
        if not self.near:
            return self
        place = lax.axis_index("seq")
        self.other_total, self.other_state = self.opened(self.moved[0])
        self.late = (place % 2 == 1) != self.reverse
        early_state = jnp.where(self.late, self.other_state, self.state)
        late_state = jnp.where(self.late, self.state, self.other_state)
        late_total = jnp.where(self.late, self.total, self.other_total)
        message = self.packed(self.total + self.other_total, self.fall(late_total) * early_state + late_state)
        sign = -1 if self.reverse else 1
        self.moved = [shifted(message, sign * 2 * k) for k in range(1, 4)]
        return self

    def result(self):
        if not self.near:
            return self.moved[0]
        got = [self.opened(v) for v in self.moved]
        carry = got[-1][1]
        for t, s in reversed(got[:-1]):
            carry = s + self.fall(t) * carry
        return jnp.where(self.late, self.fall(self.other_total) * carry + self.other_state, carry)


def seq_xor(v, bits):
    return lax.ppermute(v, "seq", [(i, i ^ bits) for i in range(lax.axis_size("seq"))])


def tied(v, *before):
    return lax.optimization_barrier((v, before))[0]


def at_index(v, index, axis):
    return lax.dynamic_index_in_dim(v, index, axis, False)


RING = (0, 2, 4, 6, 7, 5, 3, 1)


def ring_place():
    q = lax.axis_index("seq")
    return jnp.where(q % 2 == 0, q // 2, len(RING) - 1 - q // 2)


def ring_device(place):
    place = place % len(RING)
    return jnp.where(place < len(RING) // 2, 2 * place, 2 * len(RING) - 1 - 2 * place)


def ring_order():
    places = [RING.index(q) for q in range(len(RING))]
    p = ring_place()
    return [(p - k) % len(RING) for k in places] + [(k - p) % len(RING) for k in places]


class Ring:
    def __init__(self, share, between, own=None):
        self.share, self.between = share, between
        self.count, self.steps = len(RING), 0
        self.place = ring_place()
        if own is None:
            self.send([self.chunk(d, 1) for d in range(2)])
        else:
            self.steps = self.count - 1
            self.rounds = [[v] for v in own]
            self.send(own)

    def chunk(self, d, k):
        return self.share(d, ring_device(self.place + (k if d else self.count - k)))

    def send(self, held):
        self.steps += 1
        self.moving = []
        for d in range(2):
            route = [(RING[k], RING[(k + (-1 if d else 1)) % self.count]) for k in range(self.count)]
            self.moving.append(lax.ppermute(held[d], "seq", route))

    def step(self):
        k = self.steps + 1
        if k < self.count:
            self.send([self.added(d, k) for d in range(2)])
        elif k == self.count:
            own = self.between([self.added(d, k) for d in range(2)])
            self.rounds = [[v] for v in own]
            self.send(own)
        else:
            for d in range(2):
                self.rounds[d].append(self.moving[d])
            if k < 2 * self.count - 1:
                self.send(self.moving)

    def added(self, d, k):
        return (self.moving[d].astype(F32) + self.chunk(d, k).astype(F32)).astype(BF16)

    def result(self):
        return self.rounds

    def done(self):
        return self.steps >= self.count and len(self.rounds[0]) == self.count


def advance(rings, *others):
    count = 2 * len(rings)
    got = lax.optimization_barrier((*[v for ring in rings for v in ring.moving], *others))
    for i, ring in enumerate(rings):
        ring.moving = list(got[2 * i : 2 * i + 2])
        ring.step()
    return got[count] if len(others) == 1 else got[count:]


def crossed_blocks(own):
    share = [at_index(own, lax.axis_index("wsh") ^ r, 0) for r in range(own.shape[0])]
    return jnp.stack([share[0]] + [swap(share[r], r) for r in range(1, own.shape[0])])


def reduced(rows):
    return lax.psum_scatter(rows, "seq", scatter_dimension=0, tiled=True)


def local(
    hidden,
    teacher,
    cotangent,
    lengths,
    norm_gain,
    in_weight,
    conv_weight,
    conv_bias,
    x_weight,
    dt_weight,
    dt_bias,
    a_log,
    skip_gain,
    out_weight,
):
    me = lax.axis_index("wsh")
    place = lax.axis_index("seq")
    seqs = lax.axis_size("wsh")
    seq_count = lax.axis_size("seq")
    tokens, width = hidden.shape[1:]
    inner = out_weight.shape[0]
    depth = in_weight.shape[0]
    states = a_log.shape[0]
    rank = dt_weight.shape[0]
    taps = conv_weight.shape[0]
    rows = seqs * tokens

    def slots(pieces):
        return [at_index(pieces, me ^ r, 0) for r in range(seqs)]

    at = jnp.stack([place, me]).astype(jnp.int32)

    quarter = depth // 4
    half = quarter // 2
    part = place % 4

    def columns_from(start, ready):
        def block(r, first, size):
            return lax.dynamic_slice(ready, (first, start + (me ^ r) * inner), (size, inner))

        sent = [block(r, part * quarter, quarter) for r in (2, 3)]
        far = [swap(v, r) for v, r in zip(sent, (2, 3))]
        return far, [block(0, 0, depth), swap(block(1, 0, depth), 1)], sent

    def over_seq(far):
        return [seq_xor(v, bit) for bit in (1, 2) for v in far]

    def ends(by):
        return [seq_xor(v[:half], 1) for v in by[2:]] + [seq_xor(v[half:], 2) for v in by[:2]]

    x_far, x_near, x_sent = columns_from(0, in_weight)

    note = jnp.concatenate([norm_gain.astype(F32), lengths.astype(F32), jnp.zeros((127,), F32)])
    notes = jnp.stack(spread_out(tied(note, x_sent)))
    gain = jnp.concatenate(slots(notes[:, : norm_gain.shape[0]]))
    slot_lengths = notes[:, norm_gain.shape[0]]
    count = jnp.sum(jnp.minimum(slot_lengths, seq_count * tokens))
    positions = place * tokens + lax.iota(jnp.int32, tokens)
    valid = (positions[None, :].astype(F32) < slot_lengths[:, None]).astype(F32)
    halo_positions = place * tokens - HALO + lax.iota(jnp.int32, HALO + tokens)
    halo_valid = (halo_positions[None, :].astype(F32) < slot_lengths[:, None]).astype(F32)

    rows_in = hidden[0].astype(F32)
    scale = lax.rsqrt(jnp.mean(rows_in * rows_in, axis=1, keepdims=True) + NORM_EPS)
    normed_own = (rows_in * scale * gain).astype(BF16)
    before = shifted(normed_own[tokens - HALO :], 1)
    normed_own = tied(jnp.concatenate([before, normed_own], axis=0), x_far)
    normed_one, normed_two = swap(normed_own, 1), swap(normed_own, 2)
    x_by = over_seq(x_far)
    x_ends = ends(x_by)
    normed_two, x_ends = lax.optimization_barrier((normed_two, x_ends))
    normed = [normed_own, normed_one, normed_two, swap(normed_two, 1)]
    x_columns = join(at, [*x_near, *x_far, *x_by, *x_ends], width)
    z_far, z_near, _ = columns_from(seqs * inner, tied(in_weight, normed_two))
    normed = jnp.stack(normed)
    normed_tokens = normed[:, HALO:].reshape(rows, width)

    x_both = product(normed.reshape(seqs * (HALO + tokens), width), x_columns, PLAIN)
    x_in = (x_both.reshape(seqs, HALO + tokens, inner) * halo_valid[:, :, None]).astype(BF16)
    padded = x_in[:, HALO - (taps - 1) :].astype(F32)
    conv_f = conv_weight.astype(F32)
    conv_out = conv_bias.astype(F32) + sum(
        conv_f[tap] * padded[:, tap : tap + tokens] for tap in range(taps)
    )
    conv_out = conv_out.reshape(rows, inner)
    act = silu_value(conv_out).astype(BF16)
    proj = sum_all(tied(product(x_weight, act, COLS_LAST), z_far)).astype(BF16)
    dt_low = proj[:rank]
    bc = proj[rank:].astype(F32)
    step = jax.nn.softplus(product(dt_low, dt_weight, ROWS_FIRST) + dt_bias.astype(F32))
    log_rate = a_log.astype(F32)
    rate = -jnp.exp(log_rate) * LOG2E
    skip = skip_gain.astype(F32)[None]

    z_by = over_seq(tied(z_far, step))
    last_far, total_far = p1(2, step, act, bc, rate, tokens)
    z_by, last_far, total_far = lax.optimization_barrier((z_by, last_far, total_far))
    z_ends = ends(z_by)
    carry_far = Carry(total_far, last_far, rate, False)
    last_near, total_near = p1(0, tied(step, last_far), act, bc, rate, tokens)
    z_ends, last_near, total_near = carry_far.held(z_ends, last_near, total_near)
    carry_far.second()
    carry_near = Carry(total_near, last_near, rate, False)
    z_columns = join(at, [*z_near, *z_far, *z_by, *z_ends], width)
    z_part = product(normed_tokens, z_columns, PLAIN)
    z_part = carry_near.held(carry_far.held(z_part))
    carry_near.second()
    carry_far = carry_far.result()
    mixed_far, gated_far, starts_far = p2(2, step, act, z_part, bc, rate, skip, carry_far, tokens)
    mixed_far, gated_far, starts_far = carry_near.held(mixed_far, gated_far, starts_far)
    carry_near = carry_near.result()

    def parts(gated):
        return product(gated, out_weight, PLAIN).reshape(2, tokens, width)

    far = parts(gated_far)
    far = swap((far[0] + swap(far[1].astype(BF16), 1).astype(F32)).astype(BF16), 2)
    mixed_near, gated_near, starts_near = p2(0, step, act, z_part, bc, rate, skip, carry_near, tokens)
    far, gated_near = lax.optimization_barrier((far, gated_near))
    near = parts(gated_near)
    near = near[0] + swap(near[1].astype(BF16), 1).astype(F32)
    full = rows_in + near + far.astype(F32)
    own_valid = valid[0][:, None]
    miss = full - teacher[0].astype(F32)
    g_full = cotangent[0].astype(F32) + 2.0 / (width * count) * own_valid * miss
    g_own = g_full.astype(BF16)
    loss_part = jnp.sum(own_valid * miss * miss)

    g_one, g_two = swap(g_own, 1), swap(g_own, 2)
    g_branch_near = jnp.concatenate([g_own, g_one], axis=0)

    def into_mixer(g_branch, mixed, first):
        z = z_part[first * tokens : (first + 2) * tokens]
        g_gated = product(g_branch, out_weight, COLS_LAST)
        return g_gated * silu_value(z), (g_gated * mixed * silu_slope(z)).astype(BF16)

    g_mixed_near, g_z_near = into_mixer(g_branch_near, mixed_near, 0)
    first_near = b1(0, step, g_mixed_near, bc, rate, tokens)
    g_two, first_near = lax.optimization_barrier((g_two, first_near))
    back_near = Carry(total_near, first_near, rate, True)
    g_branch_far = jnp.concatenate([g_two, swap(g_two, 1)], axis=0)
    gated = jnp.concatenate([gated_near, gated_far], axis=0)
    out_grad = product(gated, jnp.concatenate([g_branch_near, g_branch_far], axis=0), ROWS_FIRST).astype(BF16)
    by_steps = seq_count == 8
    g_mixed_far, g_z_far = into_mixer(g_branch_far, mixed_far, 2)
    g_mixed_far, g_z_far = back_near.held(g_mixed_far, g_z_far)
    back_near.second()
    first_far = b1(2, step, g_mixed_far, bc, rate, tokens)
    first_far = back_near.held(first_far)
    back_near = back_near.result()
    back_far = Carry(total_far, first_far, rate, True)
    g_z = jnp.concatenate([g_z_near, g_z_far], axis=0)

    def in_shares(g, normed):
        return product(normed, g, ROWS_FIRST).astype(BF16).reshape(seqs, seq_count, depth // seq_count, g.shape[1])

    def way(v, d):
        wide = v.shape[-1] // 2
        return v[..., d * wide : (d + 1) * wide]

    def in_chunk(shares):
        return lambda d, q: at_index(way(shares, d), q, 1).reshape(width // seq_count, inner // 2)

    def in_between(own):
        return [crossed_blocks(v.reshape(seqs, -1, inner // 2)).reshape(v.shape) for v in own]

    out_own = reduced(out_grad)
    pair_near = (step, act, g_mixed_near, bc, rate, skip, starts_near, back_near, tokens)
    zero = b2(0, 1, None, *pair_near)
    zero = back_far.held(*zero)
    back_far.second()
    g_z = tied(g_z, zero)
    z_shares = jnp.swapaxes(in_shares(g_z, normed_tokens), 0, 1).reshape(width, inner)
    one = b2(1, 1, zero[:2], *pair_near)
    one = back_far.held(*one)
    back_far = back_far.result()
    z_shares, back_far = lax.optimization_barrier((z_shares, back_far))
    pair_far = (step, act, g_mixed_far, bc, rate, skip, starts_far, back_far, tokens)
    out_own, z_shares, *one = lax.optimization_barrier((out_own, z_shares, *one))
    z_own = reduced(z_shares)
    early = [Ring(None, None, [way(out_own, d) for d in range(2)])] if by_steps else []
    two = b2(2, 1, one[:2], *pair_far)
    two = advance(early, *two)
    three = b2(3, 1, two[:2], *pair_far)
    three = advance(early, *three)
    far = [*three[:2], *[jnp.concatenate([v, w]) for v, w in zip(two[2:], three[2:])]]
    near = [jnp.concatenate([v, w]) for v, w in zip(zero[2:], one[2:])]
    g_pre, g_act_part = far[:2]
    g_b, g_c = [jnp.concatenate([near[i], far[2 + i]]).reshape(rows, states).T for i in (0, 1)]
    rate_sum, sums = [jnp.sum(near[i] + far[2 + i], axis=0) for i in (2, 3)]
    dt_bias_grad, skip_grad = jnp.sum(sums, axis=1)
    g_dt_low = product(dt_weight, g_pre, COLS_LAST)
    g_proj = sum_all(
        jnp.concatenate([g_dt_low, g_b, g_c], axis=0)
    ).astype(BF16)
    g_proj = advance(early, g_proj)
    g_act = g_act_part + product(g_proj, x_weight, ROWS_FIRST)
    g_conv = (g_act * silu_slope(conv_out)).reshape(seqs, tokens, inner)
    g_padded = jnp.pad(g_conv, ((0, 0), (HALO, taps - 1), (0, 0)))
    g_x = sum(
        conv_f[tap] * g_padded[:, taps - 1 - tap : taps - 1 - tap + HALO + tokens] for tap in range(taps)
    )
    g_x = (g_x * halo_valid[:, :, None]).astype(BF16)
    conv_grad = [jnp.sum(g_conv * padded[:, tap : tap + tokens], axis=(0, 1)) for tap in range(taps)]
    small = [
        product(g_proj, act, PLAIN),
        product(dt_low, g_pre, PLAIN),
        rate_sum * (rate * LN2),
        jnp.stack(conv_grad),
        jnp.sum(g_conv, axis=(0, 1))[None],
        dt_bias_grad[None],
        skip_grad[None],
    ]
    cut = [0]
    for piece in small:
        cut.append(cut[-1] + piece.shape[0])
    lines = 16 * seq_count
    small.append(jnp.zeros((-cut[-1] % lines, inner), F32))
    small = jnp.concatenate(small, axis=0)
    normed_all = normed.reshape(seqs * (HALO + tokens), width)
    g_x_all = g_x.reshape(seqs * (HALO + tokens), inner)
    if by_steps:
        x_shares = in_shares(g_x_all, normed_all)
        small_shares = small.astype(BF16).reshape(seq_count, -1, inner)
        z_own, x_shares, small_shares, g_x = advance(early, z_own, x_shares, small_shares, g_x)
        large = width // seq_count
        chunk_of = in_chunk(x_shares)

        def x_chunk(d, q):
            return jnp.concatenate([chunk_of(d, q), at_index(way(small_shares, d), q, 0)], axis=0)

        def x_between(own):
            return [jnp.concatenate([x, v[large:]], axis=0) for x, v in zip(in_between([v[:large] for v in own]), own)]

        x_ring = Ring(x_chunk, x_between)
        out_ring = early[0]
        z_row = crossed_blocks(z_own.reshape(seqs, -1, inner)).reshape(-1, inner)
        rings = [x_ring, out_ring]
        z_row, g_x = advance(rings, z_row, g_x)
        z_ring = Ring(None, None, [way(z_row, d) for d in range(2)])
        rings.append(z_ring)
    after = shifted(g_x[:, HALO - (taps - 1) : HALO], -1)
    g_z = tied(g_z, g_x)

    def to_normed(g, columns, slot):
        return product(g[slot * tokens : (slot + 1) * tokens], columns, COLS_LAST)

    def advanced(*v):
        if by_steps:
            return advance([ring for ring in rings if not ring.done()], *v)
        return v[0] if len(v) == 1 else v

    normed_1, normed_3 = advanced(to_normed(g_z, z_columns, 1), to_normed(g_z, z_columns, 3))
    normed_2, after = advanced(to_normed(g_z, z_columns, 2), after)
    fixed = jnp.pad(after, ((0, 0), (tokens - (taps - 1), 0), (0, 0)))
    g_x = advanced((g_x[:, HALO:] + fixed).reshape(rows, inner))
    normed_1 += to_normed(g_x, x_columns, 1)
    normed_3 += to_normed(g_x, x_columns, 3)
    ready = ()
    if by_steps:
        where = jnp.stack([me] + ring_order()).astype(jnp.int32)
        out_is = partial(settle, where, out_ring.result(), out_weight.shape, 1, width)
        ready = (out_is(part=0)[0],)
    normed_1, normed_3, *ready = advanced(normed_1.astype(BF16), normed_3.astype(BF16), *ready)
    got1, got3 = swap((normed_1, normed_3), 1)
    if by_steps:
        ready = (out_is(part=1, filled=ready[0])[0],)
    got1, got3, normed_2, *ready = advanced(got1, got3, normed_2 + to_normed(g_x, x_columns, 2), *ready)
    normed_0 = advanced(to_normed(g_z, z_columns, 0))
    other = swap(tied((normed_2 + got3.astype(F32)).astype(BF16), normed_0), 2)
    normed_0 = advanced(normed_0 + to_normed(g_x, x_columns, 0) + got1.astype(F32))
    if by_steps:
        (out_owned,) = ready
        z_is = partial(settle, where, z_ring.result(), in_weight.shape, seqs, inner, half=1)
        assert out_ring.done() and z_ring.done()
        in_owned = advanced(z_is(part=0)[0])
        other, in_owned = advanced(other, z_is(part=1, filled=in_owned)[0])
    g_normed = normed_0 + other.astype(F32)
    gain_part = jnp.sum(g_normed * rows_in * scale, axis=0)
    tail = jnp.concatenate([gain_part, jnp.full((128,), loss_part)])
    if by_steps:
        for bit in (1, 2, 4):
            tail = advanced(tail + seq_xor(tail, bit))
    else:
        tail = lax.psum(tail, "seq")
    gain_share = slots(tail[:width].reshape(seqs, -1))
    gain_grad = gain_share[0] + sum(swap(gain_share[r], r) for r in range(1, seqs))
    loss_sum = tail[width:] + swap(tail[width:], 1)
    loss = (loss_sum + swap(loss_sum, 2))[0] / (width * count)
    if by_steps:
        while len(x_ring.rounds[0]) < seq_count - 1:
            in_owned = advanced(in_owned)
        blocks_of = partial(settle_some, shape=in_weight.shape, blocks=seqs, cols=inner, extra=small.shape[0])
        gap = jnp.zeros(small.shape, F32)
        for turns in ((0, 2, 3, 4, 5, 6), (1, 7)):
            devices = [ring_device(x_ring.place + seq_count - t) for t in turns]
            in_owned, gap = blocks_of(me, devices, x_ring.result(), turns, filled=(in_owned, gap))
            if not x_ring.done():
                in_owned, gap = advanced(in_owned, gap)
        small = gap
    if not by_steps:
        x_shares = jnp.swapaxes(in_shares(g_x_all, normed_all), 0, 1)
        x_row = crossed_blocks(reduced(x_shares.reshape(width, inner)).reshape(seqs, -1, inner))
        x_owned = lax.all_gather(jnp.concatenate(slots(x_row), axis=1), "seq", axis=0, tiled=True)
        small = lax.psum(small, "seq")
        out_owned = lax.all_gather(out_own, "seq", axis=0, tiled=True)
        out_owned = spread_rows([out_owned], out_weight.shape)
        in_owned = spread_rows([x_owned], in_weight.shape)
        z_row = crossed_blocks(z_own.reshape(seqs, -1, inner))
        z_owned = lax.all_gather(jnp.concatenate(slots(z_row), axis=1), "seq", axis=0, tiled=True)
        in_owned = spread_rows([z_owned], in_weight.shape, 1, in_owned)
    x_grad, dt_grad, log_rate_grad, conv_grad, conv_bias_grad, dt_bias_grad, skip_grad = cut_rows(small, cut)
    weighted = g_normed * gain
    g_rows = (
        g_full
        + scale * weighted
        - rows_in * scale * scale * scale * jnp.mean(weighted * rows_in, axis=1, keepdims=True)
    )
    return (
        full[None].astype(BF16),
        loss,
        g_rows[None].astype(BF16),
        gain_grad,
        in_owned,
        conv_grad,
        conv_bias_grad[0],
        x_grad,
        dt_grad,
        dt_bias_grad[0],
        log_rate_grad,
        skip_grad[0],
        out_owned,
    )


def solution(mesh):
    rows = P("wsh", "seq", None)
    first, second = P("wsh", None), P(None, "wsh")
    one = P("wsh")
    return jax.shard_map(
        local,
        mesh=mesh,
        in_specs=(
            rows, rows, rows, one, one, first, second, one, second, second, one, second, one, first,
        ),
        out_specs=(
            rows, P(), rows, one, first, second, one, second, second, one, second, one, first,
        ),
        check_vma=False,
    )
```
